256 devices in a mesh: req: 8 (over y, core), ep: 32 (over x, z).
Axes of the slice: x: 4, y: 4, z: 8, core: 2. Of those that a mesh axis runs over, the one named last changes fastest.
Arguments:
- queries: bfloat16 [2048, 64, 576], P(('req', 'ep')), may hold values from -7 to 7
- latent_cache: bfloat16 [256, 512, 576], P(('req', 'ep')), may hold values from -3 to 3
- new_latents: bfloat16 [2048, 576], P(('req', 'ep')), may hold values from -4 to 4
- parents: int32 [128, 16], replicated, may hold values from 0 to 14, as said below
- cache_len: int32 [128], replicated, may hold values from 128 to 1024
- tokens: bfloat16 [2048, 7168], P(('req', 'ep')), may hold values from -6 to 6
- route_ids: int32 [2048, 8], P(('req', 'ep')), may hold values from 0 to 31, all different within a row; in each aligned block of 8 rows (0 to 7, 8 to 15, ...) at most 3 rows name the same one
- route_scores: float32 [2048, 8], P(('req', 'ep')), may hold values from 0.05 to 1
- w_gate: bfloat16 [32, 7168, 2048], P('ep', None, 'req'), may hold values from -0.0625 to 0.0625
- w_up: bfloat16 [32, 7168, 2048], P('ep', None, 'req'), may hold values from -0.0625 to 0.0625
- w_down: bfloat16 [32, 2048, 7168], P('ep', 'req'), may hold values from -0.125 to 0.125
Outputs:
- attention_out: bfloat16 [2048, 64, 512], P(('req', 'ep'))
- moe_out: bfloat16 [2048, 7168], P(('req', 'ep'))
The draws below stay inside these ranges and needn't reach their ends.
Inputs may be any that keep to these rules, and one draw needn't show every extreme that they name: `route_ids`: each row names 8 different experts. Among the 8 tokens of one device (aligned blocks of 8 rows) no expert is named by more than 3 tokens, a bound that some block reaches. parents[q, 0] = 0 and parents[q, j] < j for j >= 1.
All inputs are finite; a program needn't handle non-finite values.
Results may differ from the reference program's by a relative error of at most 0.015.
Values may be sent and summed in bfloat16 or wider, within the bound.
A program may use at most 128 MiB of HBM per device.

```python
import math
import jax
import jax.numpy as jnp
import numpy as np
from jax import lax

D = 7168
FF = 2048
VDIM = 512
TOP = 8
HEADS = 64
NODES = 16
CTX = 1024
LAT = 576
TOK_DEV = 8
REQUESTS = 128
TOKENS = 2048
EXPERTS = 32
FF_DEV = 256
MOST = 3
N_REQ = 8


def joint_cache(key):
    cache_key = jax.random.fold_in(jax.random.fold_in(key, 11), 0)
    cache_shape = (REQUESTS * 2, CTX // 2, LAT)
    cache_vals = jnp.clip(jax.random.normal(cache_key, cache_shape, jnp.float32), -3.0, 3.0)
    return cache_vals


def draw_latent_cache(key, part):
    return joint_cache(key).astype(jnp.bfloat16)


def draw_queries(key, part):
    query_key = jax.random.fold_in(key, 23)
    query_shape = (REQUESTS, NODES, HEADS, LAT)
    values = jnp.clip(jax.random.normal(query_key, query_shape, jnp.float32), -6.0, 6.0)
    return values.reshape(TOKENS, HEADS, LAT).astype(jnp.bfloat16)


def draw_parents(key, part):
    offsets = jax.random.randint(jax.random.fold_in(key, 31), (REQUESTS, NODES), 0, 4)
    node_ids = jnp.arange(NODES, dtype=jnp.int32)
    parent_ids = jnp.maximum(node_ids[None, :] - 1 - offsets, 0)
    return parent_ids.at[0, NODES - 1].set(NODES - 2).astype(jnp.int32)


def draw_cache_len(key, part):
    lengths = jax.random.randint(jax.random.fold_in(key, 37), (REQUESTS,), CTX // 8, CTX + 1)
    return lengths.at[0].set(CTX).at[1].set(CTX // 8).astype(jnp.int32)


def shard_levels(stream_key, dims, cuts, least, top_value):
    def one(dim, shards_of):
        draws = jax.random.uniform(jax.random.fold_in(jax.random.fold_in(stream_key, 6), dim), (shards_of,), jnp.float32, least / len(cuts), top_value / len(cuts))
        return jnp.repeat(jnp.exp(draws), dims[dim] // shards_of).reshape((-1,) + (1,) * (len(dims) - dim - 1))

    loudness = one(*cuts[0])
    for cut in cuts[1:]:
        loudness = loudness * one(*cut)
    return loudness


def routed_block(own_key, own, number, rows, amount, top, reach, skew):
    order = jax.random.permutation(own_key, amount)
    crowded, common = shares(amount, rows * top, reach, skew, True), shares(amount, rows * top, reach, skew, False)
    places = jnp.arange(amount)

    def named(sizes, rotation):
        used = int((sizes > 0).sum())
        fixed = max(1, used // 4)
        moved = fixed + (places - fixed + rotation * (used - fixed)) % max(1, amount - fixed)
        return jnp.zeros((amount,), jnp.int32).at[order[jnp.where(places < fixed, places, moved)]].set(jnp.asarray(sizes, jnp.int32))

    sizes = jnp.where(number % 4 == 0, named(crowded, number // 4), named(common, number - number // 4 - 1))
    mixed = jax.random.permutation(jax.random.fold_in(own, 3), amount)
    donor, taker = mixed[0:amount // 2 * 2:2], mixed[1:amount // 2 * 2:2]
    margin = jnp.minimum(sizes[donor] - 1, reach - sizes[taker]) // 2
    margin = jnp.where((donor == order[0]) | (taker == order[0]) | (sizes[taker] == 0), 0, jnp.maximum(margin, 0))
    moved = jax.random.randint(jax.random.fold_in(own, 4), (amount // 2,), 0, 1 << 20) % (margin + 1)
    sizes = sizes.at[donor].add(-moved).at[taker].add(moved)
    labels = jnp.searchsorted(jnp.cumsum(sizes), jnp.arange(rows * top), side="right").astype(jnp.int32)
    table = labels.reshape(top, rows).T
    table = table[jax.random.permutation(jax.random.fold_in(own, 1), rows)]
    rotation = jax.random.randint(jax.random.fold_in(own, 2), (rows, 1), 0, top)
    return jnp.take_along_axis(table, (jnp.arange(top)[None, :] + rotation) % top, axis=1)


def shares(amount, total, limit, lean, full):
    portions = [(1 << 20) // math.isqrt(standing ** lean) + 1 for standing in range(1, amount + 1)]
    largest = limit if full else min(limit, max(-(-total // amount), total * portions[0] // sum(portions)))
    least = 1 if total - largest >= amount - 1 else 0
    given, surplus = [largest] + [least] * (amount - 1), total - largest - least * (amount - 1)
    while surplus > 0:
        movable = [i for i in range(1, amount) if given[i] < largest] or [i for i in range(1, amount) if given[i] < limit]
        pool, remaining = sum([portions[i] for i in movable]), surplus
        for i in movable:
            more = min(limit - given[i], max(1, remaining * portions[i] // pool), surplus)
            given[i] = given[i] + more
            surplus = surplus - more
    return np.array(given)


def centred(rng, extent, width, most, cuts=(), held_as=jnp.bfloat16):
    result = width * jax.random.normal(rng, extent, jnp.float32)
    if cuts:
        result = result * shard_levels(rng, extent, cuts, -0.22, 0.18)
    return jnp.clip(result, -most, most).astype(held_as)


def setup_inputs(seed: int = 0) -> dict:
    splits = jax.random.split(jax.random.key(seed), 12)
    queries = draw_queries(jax.random.fold_in(splits[11], 71), 0)
    latent_cache = draw_latent_cache(jax.random.fold_in(splits[11], 71), 0)
    new_latents = centred(splits[2], (TOKENS, LAT), 1.0, 4.0, ((0, 256),))
    parents = draw_parents(jax.random.fold_in(splits[11], 71), 0)
    cache_len = draw_cache_len(jax.random.fold_in(splits[11], 71), 0)
    tokens = centred(splits[5], (TOKENS, D), 1.0, 6.0, ((0, 256),))
    route_ids_keys = jax.random.split(jax.random.fold_in(splits[6], 1), TOKENS // TOK_DEV)
    route_ids_turns = jax.random.permutation(jax.random.fold_in(splits[6], 3), TOKENS // TOK_DEV)
    route_ids = jax.vmap(lambda own, number: routed_block(jax.random.fold_in(splits[6], 2), own, number, TOK_DEV, EXPERTS, TOP, MOST, 2))(route_ids_keys, route_ids_turns).reshape((TOKENS, TOP))
    route_scores = jnp.clip(0.05 + 0.95 * jax.random.uniform(splits[7], (TOKENS, TOP), jnp.float32) ** shard_levels(splits[7], (TOKENS, TOP), ((0, 256),), -0.2, 0.2), 0.05, 1.0)
    w_gate = centred(splits[8], (EXPERTS, D, FF), D ** -0.5, 0.0625, ((0, 32), (2, 8)))
    w_up = centred(splits[9], (EXPERTS, D, FF), D ** -0.5, 0.0625, ((0, 32), (2, 8)))
    w_down = centred(splits[10], (EXPERTS, FF, D), FF ** -0.5, 0.125, ((0, 32), (1, 8)))
    return dict(queries=queries, latent_cache=latent_cache, new_latents=new_latents, parents=parents, cache_len=cache_len, tokens=tokens, route_ids=route_ids, route_scores=route_scores, w_gate=w_gate, w_up=w_up, w_down=w_down)


score_scale = 192.0 ** -0.5
route_scale = 2.5


def ancestor_table(parent_row):
    node_count = parent_row.shape[0]
    node_ids = jnp.arange(node_count, dtype=jnp.int32)
    current = node_ids
    visible = node_ids[:, None] == node_ids[None, :]
    for repeat in range(node_count):
        current = parent_row[current]
        visible = visible | (current[:, None] == node_ids[None, :])
    return visible


def attend_request(operands):
    query_rows, cache_rows, fresh_rows, parent_row, length = operands
    context = cache_rows.shape[0] * cache_rows.shape[1]
    key_rows = jnp.concatenate([cache_rows.reshape(context, cache_rows.shape[2]), fresh_rows], axis=0)
    scores = jnp.einsum("nhl,kl->nhk", query_rows.astype(jnp.float32), key_rows.astype(jnp.float32)) * score_scale
    cached = jnp.arange(context, dtype=jnp.int32) < length
    tree_vis = ancestor_table(parent_row)
    visible = jnp.concatenate([jnp.broadcast_to(cached[None, :], (tree_vis.shape[0], context)), tree_vis], axis=1)
    masked = jnp.where(visible[:, None, :], scores, -jnp.inf)
    row_max = jnp.max(masked, axis=-1, keepdims=True)
    shifted = jnp.exp(masked - row_max)
    attn_probs = (shifted / jnp.sum(shifted, axis=-1, keepdims=True)).astype(jnp.bfloat16)
    value_rows = key_rows[:, :VDIM]
    return jnp.einsum("nhk,kv->nhv", attn_probs.astype(jnp.float32), value_rows.astype(jnp.float32)).astype(jnp.bfloat16)


def reference(queries, latent_cache, new_latents, parents, cache_len, tokens, route_ids, route_scores, w_gate, w_up, w_down):
    query_group = queries.reshape(REQUESTS, NODES, HEADS, LAT)
    cache_group = latent_cache.reshape(REQUESTS, 2, CTX // 2, LAT)
    fresh_group = new_latents.reshape(REQUESTS, NODES, LAT)
    attended = lax.map(attend_request, (query_group, cache_group, fresh_group, parents, cache_len))
    attention_out = attended.reshape(TOKENS, HEADS, VDIM)

    route_weight = route_scale * route_scores / jnp.sum(route_scores, axis=1, keepdims=True)
    blocks = TOKENS // TOK_DEV
    block_ids = route_ids.reshape(blocks, TOK_DEV * TOP)
    onehot = (block_ids[:, :, None] == jnp.arange(EXPERTS, dtype=jnp.int32)[None, None, :]).astype(jnp.int32)
    slot_rank = jnp.sum(jnp.cumsum(onehot, axis=1) * onehot, axis=2) - 1
    slot_of = block_ids * (blocks * MOST) + jnp.arange(blocks, dtype=jnp.int32)[:, None] * MOST + slot_rank
    token_of_pair = jnp.arange(TOKENS * TOP, dtype=jnp.int32) // TOP
    table_size = EXPERTS * blocks * MOST
    token_table = jnp.zeros((table_size,), jnp.int32).at[slot_of.reshape(-1)].set(token_of_pair)
    weight_table = jnp.zeros((table_size,), jnp.float32).at[slot_of.reshape(-1)].set(route_weight.reshape(-1))
    token_table = token_table.reshape(EXPERTS, blocks * MOST)
    weight_table = weight_table.reshape(EXPERTS, blocks * MOST)

    def one_expert(running, operands):
        gate_mat, up_mat, down_mat, token_rows, row_weights = operands
        picked = tokens[token_rows]
        gate_val = jnp.dot(picked, gate_mat, preferred_element_type=jnp.float32)
        up_val = jnp.dot(picked, up_mat, preferred_element_type=jnp.float32)
        hidden = (jax.nn.silu(gate_val) * up_val).astype(jnp.bfloat16)
        pieces = hidden.reshape(hidden.shape[0], N_REQ, FF_DEV)
        partial_value = jnp.einsum("rnf,nfd->nrd", pieces.astype(jnp.float32), down_mat.reshape(N_REQ, FF_DEV, D).astype(jnp.float32)).astype(jnp.bfloat16)
        expert_out = jnp.sum(partial_value.astype(jnp.float32), axis=0)
        return running.at[token_rows].add(expert_out * row_weights[:, None]), None

    running, unused = lax.scan(one_expert, jnp.zeros((TOKENS, D), jnp.float32), (w_gate, w_up, w_down, token_table, weight_table))
    moe_out = running.astype(jnp.bfloat16)
    return attention_out, moe_out
```

```python
import functools

import jax
import jax.numpy as jnp
from jax import lax
from jax.experimental import pallas as pl
from jax.experimental.pallas import tpu as pltpu
from jax.sharding import PartitionSpec as P

VDIM = 512
NX, NZ, NY, NC = 4, 8, 4, 2
CAP = 3
PAD = 4
CHUNKS = 7

score_scale = 192.0 ** (-0.5)
route_scale = 2.5
F32, BF16 = jnp.float32, jnp.bfloat16
MESH = pl.DeviceIdType.MESH


def iota(shape, dim):
    return lax.broadcasted_iota(jnp.int32, shape, dim)


def mm(a, b):
    return jnp.dot(a, b, preferred_element_type=F32)


def mm_nt(a, b):
    return lax.dot_general(a, b, (((1,), (1,)), ((), ())), preferred_element_type=F32)


def kernel(
    tok, rid, rsc, queries, cache, newlat, parents, clen, wg_h, wu_h, wd_h,
    attn_out, moe_out,
    wg, wu, wd, qbuf, cachebuf, fresh, vis, obuf,
    msend, metabuf, smat, pmat, emat, whi, wlo,
    zbuf, xsend, xbuf, ybuf, gacc, uacc, act,
    dsend, drecv, r1send, r1recv, r2send, r2recv, x2send, x2buf, z2send, z2buf,
    loc_sem, out_sem, c_send, c_recv, m_send, m_recv,
    z_send, z_recv, x_send, x_recv, y_send, y_recv, s_send, s_recv,
    d_send, d_recv, r1_send, r1_recv, r2_send, r2_recv, x2_send, x2_recv, z2_send, z2_recv,
):
    req, ep = lax.axis_index("req"), lax.axis_index("ep")
    my_y, my_c = req // NC, req % NC
    my_x, my_z = ep // NZ, ep % NZ
    K = CHUNKS
    T = tok.shape[0]
    C = tok.shape[1] // K
    S = NZ * PAD
    R = NX * NZ * CAP
    HR = R // 2
    FF = wg.shape[1]
    rot = lambda a, j, n: lax.rem(a + j + n, n)
    nxt, prv, far = rot(my_y, 1, NY), rot(my_y, -1, NY), rot(my_y, 2, NY)
    dev_y = lambda y: (y * NC + my_c, ep)
    dev_x = lambda x: (req, x * NZ + my_z)
    dev_z = lambda z: (req, my_x * NZ + z)
    sib = (my_y * NC + (1 - my_c), ep)
    blk_of = lambda y: my_c * NY + y
    half = ep % 2
    mate = (req, ep + 1 - 2 * half)
    cols = lambda k: pl.ds(pl.multiple_of(k * C, 128), C)

    def remote(src, dst, ssem, rsem, device):
        return pltpu.make_async_remote_copy(
            src_ref=src, dst_ref=dst, send_sem=ssem, recv_sem=rsem,
            device_id=device, device_id_type=MESH,
        )

    def meta_copy(j):
        return remote(msend, metabuf.at[my_z], m_send.at[j - 1], m_recv.at[j - 1],
                      dev_z(rot(my_z, j, NZ)))

    def z_copy(k, j):
        return remote(tok.at[:, cols(k)], zbuf.at[k, my_z], z_send.at[k, j - 1],
                      z_recv.at[k, j - 1], dev_z(rot(my_z, j, NZ)))

    def x_copy(k, j):
        to = rot(my_x, j, NX)
        return remote(xsend.at[k, to], xbuf.at[k, my_x], x_send.at[k, j - 1],
                      x_recv.at[k, j - 1], dev_x(to))

    def y_copy(k, i):
        if i < 2:
            ref = ybuf.at[k, blk_of(my_y)]
        elif i == 2:
            ref = ybuf.at[k, blk_of(prv), pl.ds(0, HR)]
        else:
            ref = ybuf.at[k, blk_of(nxt), pl.ds(HR, HR)]
        return remote(ref, ref, y_send.at[k, i], y_recv.at[k, i],
                      dev_y(nxt if i % 2 == 0 else prv))

    def s_copy(k, i):
        ref = ybuf.at[k, blk_of((my_y, prv, nxt, far)[i])]
        return remote(ref, ref, s_send.at[k, i], s_recv.at[k, i], sib)

    def d_copy(k):
        return remote(dsend.at[k], drecv.at[k], d_send.at[k], d_recv.at[k], sib)

    def r1_copy(k, i):
        return remote(r1send.at[k, i], r1recv.at[k, i], r1_send.at[k, i], r1_recv.at[k, i],
                      dev_y(nxt if i == 0 else prv))

    def r2_copy(k, i):
        return remote(r2send.at[k, i], r2recv.at[k, i], r2_send.at[k, i], r2_recv.at[k, i],
                      dev_y(nxt if i == 0 else prv))

    def x2_copy(k, j):
        to = rot(my_x, j, NX)
        return remote(x2send.at[k, to], x2buf.at[k, my_x], x2_send.at[k, j - 1],
                      x2_recv.at[k, j - 1], dev_x(to))

    def z2_copy(k, j):
        to = rot(my_z, j, NZ)
        return remote(z2send.at[k, to], z2buf.at[k, my_z], z2_send.at[k, j - 1],
                      z2_recv.at[k, j - 1], dev_z(to))

    cache_copy = remote(cache.at[0], cachebuf.at[half], c_send.at[0], c_recv.at[0], mate)
    fresh_copy = remote(newlat, fresh.at[half], c_send.at[1], c_recv.at[1], mate)
    local = [
        pltpu.make_async_copy(wg_h.at[0], wg, loc_sem.at[0]),
        pltpu.make_async_copy(wu_h.at[0], wu, loc_sem.at[1]),
        pltpu.make_async_copy(wd_h.at[0], wd, loc_sem.at[2]),
        pltpu.make_async_copy(queries, qbuf, loc_sem.at[3]),
        pltpu.make_async_copy(cache.at[0], cachebuf.at[half], loc_sem.at[4]),
    ]

    barrier = pltpu.get_barrier_semaphore()
    peers = [dev_z(rot(my_z, j, NZ)) for j in range(1, NZ)]
    peers += [dev_x(rot(my_x, j, NX)) for j in range(1, NX)]
    peers += [dev_y(nxt), dev_y(prv), sib]
    for peer in peers:
        pl.semaphore_signal(barrier, inc=1, device_id=peer, device_id_type=MESH)
    msend[...] = jnp.zeros_like(msend)
    msend[0:T, 0:rid.shape[1]] = rid[...].astype(F32)
    scores = rsc[...]
    msend[T:2 * T, 0:rid.shape[1]] = route_scale * scores / jnp.sum(scores, axis=1, keepdims=True)
    metabuf[my_z] = msend[...]
    pl.semaphore_wait(barrier, len(peers))

    def z_start(k):
        for j in range(1, NZ):
            z_copy(k, j).start()
        zbuf[k, my_z] = tok[:, cols(k)]

    for j in range(1, NZ):
        meta_copy(j).start()
    z_start(0)
    z_start(1)
    for copy in local:
        copy.start()
    fresh[half] = newlat[...]

    gacc[...] = jnp.zeros_like(gacc)
    uacc[...] = jnp.zeros_like(uacc)
    XS = NX * S
    c_row, p_col = iota((R, XS), 1), iota((R, XS), 0)
    place = (c_row // S) * (NZ * CAP) + ((c_row % S) // PAD) * CAP + c_row % PAD
    pmat[...] = jnp.where((place == p_col) & (c_row % PAD < CAP), 1.0, 0.0).astype(BF16)
    c_row, p_col = iota((XS, R), 0), iota((XS, R), 1)
    place = (c_row // S) * (NZ * CAP) + ((c_row % S) // PAD) * CAP + c_row % PAD
    emat[...] = jnp.where((place == p_col) & (c_row % PAD < CAP), 1.0, 0.0).astype(BF16)

    request = (req * (NX * NZ) + ep) // 2
    nodes = parents.shape[1]
    par = parents[pl.ds(request, 1), :]
    par = jnp.concatenate([par, jnp.full((1, 128 - nodes), -1, jnp.int32)], axis=1)
    down, across = iota((128, 128), 0), iota((128, 128), 1)
    reach = jnp.where((down == across) | (down == par), 1.0, 0.0)
    for _ in range(4):
        reach = jnp.minimum(mm(reach.astype(BF16), reach.astype(BF16)), 1.0)
    vis[...] = jnp.transpose(reach)[0:2 * T]

    for j in range(1, NZ):
        meta_copy(j).wait_recv()
    L = NZ * T
    ids = jnp.concatenate([metabuf[z, 0:T] for z in range(NZ)], axis=0)
    wts = jnp.concatenate([metabuf[z, T:2 * T] for z in range(NZ)], axis=0)
    slot, line = iota((L, XS), 1), iota((L, XS), 0)
    expert = ((slot // S) * NZ + my_z).astype(F32)
    named, weight = jnp.zeros((L, XS), F32), jnp.zeros((L, XS), F32)
    for top in range(rid.shape[1]):
        hit = ids[:, top:top + 1] == expert
        named = jnp.where(hit, 1.0, named)
        weight = jnp.where(hit, wts[:, top:top + 1], weight)
    r0, r1 = iota((L, L), 0), iota((L, L), 1)
    before = jnp.where((r0 // T == r1 // T) & (r1 < r0), 1.0, 0.0).astype(BF16)
    rank = mm(before, named.astype(BF16))
    mine = (named > 0.5) & ((slot % S) // PAD == line // T) & (rank == (slot % PAD).astype(F32))
    smat[...] = jnp.transpose(jnp.where(mine, 1.0, 0.0)).astype(BF16)
    weight = jnp.where(mine, weight, 0.0)
    high = weight.astype(BF16)
    whi[...] = high
    wlo[...] = (weight - high.astype(F32)).astype(BF16)

    def select(k):
        for j in range(1, NZ):
            z_copy(k, j).wait_recv()
        rows = jnp.concatenate([zbuf[k, z].astype(F32) for z in range(NZ)], axis=0).astype(BF16)
        picked = mm(smat[...], rows).astype(BF16)
        for x in range(NX):
            xsend[k, x] = picked[x * S:(x + 1) * S]
        for j in range(1, NX):
            x_copy(k, j).start()
        xbuf[k, my_x] = xsend[k, my_x]

    def gather_own(k):
        for j in range(1, NX):
            x_copy(k, j).wait_recv()
        rows = jnp.concatenate([xbuf[k, x] for x in range(NX)], axis=0)
        ybuf[k, blk_of(my_y)] = mm(pmat[...], rows).astype(BF16)
        y_copy(k, 0).start()
        y_copy(k, 1).start()
        s_copy(k, 0).start()

    def gather_near(k):
        y_copy(k, 0).wait_recv()
        y_copy(k, 2).start()
        s_copy(k, 1).start()
        y_copy(k, 1).wait_recv()
        y_copy(k, 3).start()
        s_copy(k, 2).start()

    def gather_far(k):
        y_copy(k, 2).wait_recv()
        y_copy(k, 3).wait_recv()
        s_copy(k, 3).start()

    def multiply_up(k):
        for i in range(4):
            s_copy(k, i).wait_recv()
        w_rows = pl.ds(pl.multiple_of(k * C, 128), C)

        def rows_of(i, _):
            rows = ybuf[k, pl.ds(2 * i, 2)].reshape(2 * R, C)
            at = pl.ds(pl.multiple_of(i * 2 * R, 8), 2 * R)
            gacc[at] += mm(rows, wg[w_rows])
            uacc[at] += mm(rows, wu[w_rows])
            return 0

        lax.fori_loop(0, NC * NY // 2, rows_of, 0)

    heads = qbuf.shape[1]
    ctx = cachebuf.shape[0] * cachebuf.shape[1]
    length = clen[request]

    def attend(i):
        q = qbuf[pl.ds(2 * i, 2)].reshape(2 * heads, qbuf.shape[2])
        keys = cachebuf[...].reshape(ctx, cachebuf.shape[2])
        near = jnp.concatenate([fresh[0].astype(F32), fresh[1].astype(F32)], axis=0).astype(BF16)
        s_far = mm_nt(q, keys) * score_scale
        s_near = mm_nt(q, near) * score_scale
        s_far = jnp.where(iota((2 * heads, ctx), 1) < length, s_far, -jnp.inf)
        seen = jnp.concatenate(
            [
                jnp.broadcast_to(vis[pl.ds(half * T + 2 * i + n, 1), :], (heads, 128))
                for n in range(2)
            ],
            axis=0,
        )[:, :2 * T]
        s_near = jnp.where(seen > 0.5, s_near, -jnp.inf)
        top = jnp.maximum(
            jnp.max(s_far, axis=1, keepdims=True), jnp.max(s_near, axis=1, keepdims=True)
        )
        p_far, p_near = jnp.exp(s_far - top), jnp.exp(s_near - top)
        total = jnp.sum(p_far, axis=1, keepdims=True) + jnp.sum(p_near, axis=1, keepdims=True)
        p_far, p_near = (p_far / total).astype(BF16), (p_near / total).astype(BF16)
        out = mm(p_far, keys[:, :VDIM]) + mm(p_near, near[:, :VDIM])
        obuf[pl.ds(2 * i, 2)] = out.astype(BF16).reshape(2, heads, VDIM)

    pieces = T // 2
    first_piece = K + 3 - pieces - 1

    def dispatch_step(s, _):
        @pl.when(s + 2 < K)
        def _():
            z_start(s + 2)

        @pl.when(s == 1)
        def _():
            cache_copy.start()
            fresh_copy.start()

        @pl.when(s < K)
        def _():
            select(s)

        @pl.when((s >= 1) & (s < K + 1))
        def _():
            gather_own(s - 1)

        @pl.when((s >= 2) & (s < K + 2))
        def _():
            gather_near(s - 2)

        @pl.when(s == 3)
        def _():
            local[0].wait()
            local[1].wait()

        @pl.when(s == first_piece)
        def _():
            local[3].wait()
            local[4].wait()
            cache_copy.wait_recv()
            fresh_copy.wait_recv()

        @pl.when((s >= first_piece) & (s < first_piece + pieces))
        def _():
            attend(s - first_piece)

        @pl.when(s >= 3)
        def _():
            gather_far(s - 3)
            multiply_up(s - 3)

        return 0

    lax.fori_loop(0, K + 3, dispatch_step, 0)

    out_copy = pltpu.make_async_copy(obuf, attn_out, out_sem)
    out_copy.start()
    gate = gacc[...]
    act[...] = (gate / (1.0 + jnp.exp(-gate)) * uacc[...]).astype(BF16).reshape(act.shape)
    local[2].wait()

    def down_other(k):
        rows = act[1 - my_c].reshape(NY * R, FF)
        dsend[k] = mm(rows, wd[:, cols(k)]).astype(BF16).reshape(NY, R, C)
        d_copy(k).start()

    def own_rows(k, y):
        return mm(act[my_c, y], wd[:, cols(k)]) + drecv[k, y].astype(F32)

    def send_far(k):
        d_copy(k).wait_recv()
        rows = own_rows(k, far).astype(BF16)
        r1send[k, 0] = rows[:HR]
        r1_copy(k, 0).start()
        r1send[k, 1] = rows[HR:]
        r1_copy(k, 1).start()

    def send_near(k):
        r1_copy(k, 0).wait_recv()
        rows = own_rows(k, nxt)
        more = r1recv[k, 0].astype(F32)
        r2send[k, 0] = jnp.concatenate([rows[:HR] + more, rows[HR:]], axis=0).astype(BF16)
        r2_copy(k, 0).start()
        r1_copy(k, 1).wait_recv()
        rows = own_rows(k, prv)
        more = r1recv[k, 1].astype(F32)
        r2send[k, 1] = jnp.concatenate([rows[:HR], rows[HR:] + more], axis=0).astype(BF16)
        r2_copy(k, 1).start()

    def send_back(k):
        rows = own_rows(k, my_y)
        r2_copy(k, 0).wait_recv()
        r2_copy(k, 1).wait_recv()
        rows = (rows + r2recv[k, 0].astype(F32) + r2recv[k, 1].astype(F32)).astype(BF16)
        spread = mm(emat[...], rows).astype(BF16)
        for x in range(NX):
            x2send[k, x] = spread[x * S:(x + 1) * S]
        for j in range(1, NX):
            x2_copy(k, j).start()
        x2buf[k, my_x] = x2send[k, my_x]

    def weigh(k):
        for j in range(1, NX):
            x2_copy(k, j).wait_recv()
        rows = jnp.concatenate([x2buf[k, x] for x in range(NX)], axis=0)
        sums = (mm(whi[...], rows) + mm(wlo[...], rows)).astype(BF16)
        for z in range(NZ):
            z2send[k, z] = sums[z * T:(z + 1) * T]
        for j in range(1, NZ):
            z2_copy(k, j).start()
        z2buf[k, my_z] = z2send[k, my_z]

    def finish(k):
        for j in range(1, NZ):
            z2_copy(k, j).wait_recv()
        rows = z2buf[k, 0].astype(F32)
        for z in range(1, NZ):
            rows = rows + z2buf[k, z].astype(F32)
        moe_out[:, cols(k)] = rows.astype(BF16)

    def sent_dispatch(k):
        for j in range(1, NZ):
            z_copy(k, j).wait_send()
        for j in range(1, NX):
            x_copy(k, j).wait_send()
        for i in range(4):
            y_copy(k, i).wait_send()
            s_copy(k, i).wait_send()

    def sent_combine(k):
        d_copy(k).wait_send()
        for i in range(2):
            r1_copy(k, i).wait_send()
            r2_copy(k, i).wait_send()
        for j in range(1, NX):
            x2_copy(k, j).wait_send()
        for j in range(1, NZ):
            z2_copy(k, j).wait_send()

    def combine_step(s, _):
        @pl.when(s < K)
        def _():
            down_other(s)

        @pl.when((s >= 1) & (s < K + 1))
        def _():
            send_far(s - 1)
            sent_dispatch(s - 1)

        @pl.when((s >= 2) & (s < K + 2))
        def _():
            send_near(s - 2)

        @pl.when((s >= 3) & (s < K + 3))
        def _():
            send_back(s - 3)

        @pl.when((s >= 4) & (s < K + 4))
        def _():
            weigh(s - 4)

        @pl.when(s >= 5)
        def _():
            finish(s - 5)
            sent_combine(s - 5)

        return 0

    lax.fori_loop(0, K + 5, combine_step, 0)
    for j in range(1, NZ):
        meta_copy(j).wait_send()
    cache_copy.wait_send()
    fresh_copy.wait_send()
    out_copy.wait()


def body(queries, cache, newlat, parents, clen, tok, rid, rsc, wg, wu, wd):
    T, D = tok.shape
    K = CHUNKS
    C = D // K
    S, R = NZ * PAD, NX * NZ * CAP
    HR = R // 2
    heads, lat = queries.shape[1:]
    FF = wg.shape[2]
    n_rows = NC * NY * R
    vmem, dma = pltpu.VMEM, pltpu.SemaphoreType.DMA
    anyspec, vspec = pl.BlockSpec(memory_space=pl.ANY), pl.BlockSpec(memory_space=pltpu.VMEM)
    scratch = [
        vmem((D, FF), BF16), vmem((D, FF), BF16), vmem((FF, D), BF16),
        vmem((T, heads, lat), BF16), vmem((2, cache.shape[1], lat), BF16),
        vmem((2, T, lat), BF16), vmem((2 * T, 128), F32), vmem((T, heads, VDIM), BF16),
        vmem((2 * T, 128), F32), vmem((NZ, 2 * T, 128), F32),
        vmem((NX * S, NZ * T), BF16), vmem((R, NX * S), BF16), vmem((NX * S, R), BF16),
        vmem((NZ * T, NX * S), BF16), vmem((NZ * T, NX * S), BF16),
        vmem((K, NZ, T, C), BF16), vmem((K, NX, S, C), BF16), vmem((K, NX, S, C), BF16),
        vmem((K, NC * NY, R, C), BF16), vmem((n_rows, FF), F32), vmem((n_rows, FF), F32),
        vmem((NC, NY, R, FF), BF16),
        vmem((K, NY, R, C), BF16), vmem((K, NY, R, C), BF16),
        vmem((K, 2, HR, C), BF16), vmem((K, 2, HR, C), BF16),
        vmem((K, 2, R, C), BF16), vmem((K, 2, R, C), BF16),
        vmem((K, NX, S, C), BF16), vmem((K, NX, S, C), BF16),
        vmem((K, NZ, T, C), BF16), vmem((K, NZ, T, C), BF16),
        dma((5,)), dma, dma((2,)), dma((2,)), dma((NZ - 1,)), dma((NZ - 1,)),
        dma((K, NZ - 1)), dma((K, NZ - 1)), dma((K, NX - 1)), dma((K, NX - 1)),
        dma((K, 4)), dma((K, 4)), dma((K, 4)), dma((K, 4)),
        dma((K,)), dma((K,)), dma((K, 2)), dma((K, 2)), dma((K, 2)), dma((K, 2)),
        dma((K, NX - 1)), dma((K, NX - 1)), dma((K, NZ - 1)), dma((K, NZ - 1)),
    ]
    flops = 2 * n_rows * D * FF * 3 + 2 * T * heads * 2 * cache.shape[1] * (lat + VDIM)
    return tuple(pl.pallas_call(
        kernel,
        out_shape=(
            jax.ShapeDtypeStruct((T, heads, VDIM), BF16),
            jax.ShapeDtypeStruct((T, D), BF16),
        ),
        in_specs=[
            vspec, vspec, vspec, anyspec, anyspec, vspec, vspec,
            pl.BlockSpec(memory_space=pltpu.SMEM), anyspec, anyspec, anyspec,
        ],
        out_specs=(anyspec, vspec),
        scratch_shapes=scratch,
        compiler_params=pltpu.CompilerParams(
            collective_id=0, has_side_effects=True, vmem_limit_bytes=63 * 1024 * 1024
        ),
        cost_estimate=pl.CostEstimate(flops=flops, bytes_accessed=14_000_000, transcendentals=0),
        name="verify_layer",
    )(tok, rid, rsc, queries, cache, newlat, parents, clen, wg, wu, wd))


def solution(mesh):
    placed = (
        P(("req", "ep"), None, None),
        P(("req", "ep"), None, None),
        P(("req", "ep"), None),
        P(),
        P(),
        P(("req", "ep"), None),
        P(("req", "ep"), None),
        P(("req", "ep"), None),
        P("ep", None, "req"),
        P("ep", None, "req"),
        P("ep", "req", None),
    )
    return jax.shard_map(
        body,
        mesh=mesh,
        in_specs=placed,
        out_specs=(P(("req", "ep"), None, None), P(("req", "ep"), None)),
        check_vma=False,
    )
```

```python
import functools

import jax
import jax.numpy as jnp
from jax import lax
from jax.experimental import pallas as pl
from jax.experimental.pallas import tpu as pltpu
from jax.sharding import PartitionSpec as P

VDIM = 512
NX, NZ, NY, NC = 4, 8, 4, 2
CAP = 3
PAD = 4
CHUNKS = 7
LEAD, NEAR, FAR = 2, 2, 3
COMB_FAR, COMB_NEAR, COMB_BACK, COMB_WEIGH, COMB_END = 1, 2, 3, 4, 5
CACHE_AT, ATTEND_AT = 5, 3

score_scale = 192.0 ** (-0.5)
route_scale = 2.5
F32, BF16 = jnp.float32, jnp.bfloat16
MESH = pl.DeviceIdType.MESH


def iota(shape, dim):
    return lax.broadcasted_iota(jnp.int32, shape, dim)


def mm(a, b):
    return jnp.dot(a, b, preferred_element_type=F32)


def mm_nt(a, b):
    return lax.dot_general(a, b, (((1,), (1,)), ((), ())), preferred_element_type=F32)


def kernel(
    tok, rid, rsc, queries, cache, newlat, parents, clen, wg_h, wu_h, wd_h,
    attn_out, moe_out,
    wg, wu, wd, qbuf, cachebuf, fresh, vis, obuf,
    msend, metabuf, smat, pmat, emat, whi, wlo,
    zbuf, xsend, xbuf, ybuf, gacc, uacc, act,
    dsend, drecv, r1send, r1recv, r2send, r2recv, x2send, x2buf, z2send, z2buf,
    loc_sem, out_sem, c_send, c_recv, m_send, m_recv,
    z_send, z_recv, x_send, x_recv, y_send, y_recv, s_send, s_recv,
    d_send, d_recv, r1_send, r1_recv, r2_send, r2_recv, x2_send, x2_recv, z2_send, z2_recv,
):
    req, ep = lax.axis_index("req"), lax.axis_index("ep")
    my_y, my_c = req // NC, req % NC
    my_x, my_z = ep // NZ, ep % NZ
    K = CHUNKS
    T = tok.shape[0]
    C = tok.shape[1] // K
    S = NZ * PAD
    R = NX * NZ * CAP
    HR = R // 2
    FF = wg.shape[1]
    rot = lambda a, j, n: lax.rem(a + j + n, n)
    nxt, prv, far = rot(my_y, 1, NY), rot(my_y, -1, NY), rot(my_y, 2, NY)
    dev_y = lambda y: (y * NC + my_c, ep)
    dev_x = lambda x: (req, x * NZ + my_z)
    dev_z = lambda z: (req, my_x * NZ + z)
    sib = (my_y * NC + (1 - my_c), ep)
    blk_of = lambda y: my_c * NY + y
    half = ep % 2
    mate = (req, ep + 1 - 2 * half)
    cols = lambda k: pl.ds(pl.multiple_of(k * C, 128), C)

    def remote(src, dst, ssem, rsem, device):
        return pltpu.make_async_remote_copy(
            src_ref=src, dst_ref=dst, send_sem=ssem, recv_sem=rsem,
            device_id=device, device_id_type=MESH,
        )

    def meta_copy(j):
        return remote(msend, metabuf.at[my_z], m_send, m_recv,
                      dev_z(rot(my_z, j, NZ)))

    def z_copy(k, j):
        return remote(tok.at[:, cols(k)], zbuf.at[k, my_z], z_send,
                      z_recv.at[k], dev_z(rot(my_z, j, NZ)))

    def x_copy(k, j):
        to = rot(my_x, j, NX)
        return remote(xsend.at[k, to], xbuf.at[k, my_x], x_send,
                      x_recv.at[k], dev_x(to))

    def y_copy(k, i):
        if i < 2:
            ref = ybuf.at[k, blk_of(my_y)]
        elif i == 2:
            ref = ybuf.at[k, blk_of(prv), pl.ds(0, HR)]
        else:
            ref = ybuf.at[k, blk_of(nxt), pl.ds(HR, HR)]
        return remote(ref, ref, y_send, y_recv.at[k, i // 2],
                      dev_y(nxt if i % 2 == 0 else prv))

    def s_copy(k, i):
        ref = ybuf.at[k, blk_of((my_y, prv, nxt, far)[i])]
        return remote(ref, ref, s_send, s_recv.at[k], sib)

    def d_copy(k, i):
        part = pl.ds(0, 1) if i == 0 else pl.ds(1, NY - 1)
        return remote(dsend.at[k, part], drecv.at[k, part], d_send, d_recv.at[k, i], sib)

    def r1_copy(k, i):
        return remote(r1send.at[k, i], r1recv.at[k, i], r1_send, r1_recv.at[k],
                      dev_y(nxt if i == 0 else prv))

    def r2_copy(k, i):
        return remote(r2send.at[k, i], r2recv.at[k, i], r2_send, r2_recv.at[k],
                      dev_y(nxt if i == 0 else prv))

    def x2_copy(k, j):
        to = rot(my_x, j, NX)
        return remote(x2send.at[k, to], x2buf.at[k, my_x], x2_send,
                      x2_recv.at[k], dev_x(to))

    def z2_copy(k, j):
        to = rot(my_z, j, NZ)
        return remote(z2send.at[k, to], z2buf.at[k, my_z], z2_send,
                      z2_recv.at[k], dev_z(to))

    def bytes_of(ref, sem):
        pltpu.make_async_copy(ref, ref, sem).wait()

    cache_copy = remote(cache.at[0], cachebuf.at[half], c_send.at[0], c_recv.at[0], mate)
    fresh_copy = remote(newlat, fresh.at[half], c_send.at[1], c_recv.at[1], mate)
    local = [
        pltpu.make_async_copy(wg_h.at[0], wg, loc_sem.at[0]),
        pltpu.make_async_copy(wu_h.at[0], wu, loc_sem.at[1]),
        pltpu.make_async_copy(wd_h.at[0], wd, loc_sem.at[2]),
        pltpu.make_async_copy(queries, qbuf, loc_sem.at[3]),
        pltpu.make_async_copy(cache.at[0], cachebuf.at[half], loc_sem.at[4]),
    ]

    barrier = pltpu.get_barrier_semaphore()
    peers = [dev_z(rot(my_z, j, NZ)) for j in range(1, NZ)]
    peers += [dev_x(rot(my_x, j, NX)) for j in range(1, NX)]
    peers += [dev_y(nxt), dev_y(prv), sib]
    for peer in peers:
        pl.semaphore_signal(barrier, inc=1, device_id=peer, device_id_type=MESH)
    msend[...] = jnp.zeros_like(msend)
    msend[0:T, 0:rid.shape[1]] = rid[...].astype(F32)
    scores = rsc[...]
    msend[T:2 * T, 0:rid.shape[1]] = route_scale * scores / jnp.sum(scores, axis=1, keepdims=True)
    metabuf[my_z] = msend[...]
    for copy in local:
        copy.start()
    fresh[half] = newlat[...]
    XS = NX * S
    c_row, p_col = iota((R, XS), 1), iota((R, XS), 0)
    place = (c_row // S) * (NZ * CAP) + ((c_row % S) // PAD) * CAP + c_row % PAD
    pmat[...] = jnp.where((place == p_col) & (c_row % PAD < CAP), 1.0, 0.0).astype(BF16)
    pl.semaphore_wait(barrier, len(peers))

    def z_start(k):
        for j in range(1, NZ):
            z_copy(k, j).start()
        zbuf[k, my_z] = tok[:, cols(k)]

    for j in range(1, NZ):
        meta_copy(j).start()
    for k in range(LEAD):
        z_start(k)

    bytes_of(metabuf.at[pl.ds(0, NZ - 1)], m_recv)
    L = NZ * T
    ids = jnp.concatenate([metabuf[z, 0:T] for z in range(NZ)], axis=0)
    wts = jnp.concatenate([metabuf[z, T:2 * T] for z in range(NZ)], axis=0)
    slot, line = iota((L, XS), 1), iota((L, XS), 0)
    expert = ((slot // S) * NZ + my_z).astype(F32)
    named, weight = jnp.zeros((L, XS), F32), jnp.zeros((L, XS), F32)
    for top in range(rid.shape[1]):
        hit = ids[:, top:top + 1] == expert
        named = jnp.where(hit, 1.0, named)
        weight = jnp.where(hit, wts[:, top:top + 1], weight)
    r0, r1 = iota((L, L), 0), iota((L, L), 1)
    before = jnp.where((r0 // T == r1 // T) & (r1 < r0), 1.0, 0.0).astype(BF16)
    rank = mm(before, named.astype(BF16))
    mine = (named > 0.5) & ((slot % S) // PAD == line // T) & (rank == (slot % PAD).astype(F32))
    smat[...] = jnp.transpose(jnp.where(mine, 1.0, 0.0)).astype(BF16)
    weight = jnp.where(mine, weight, 0.0)
    high = weight.astype(BF16)
    whi[...] = high
    wlo[...] = (weight - high.astype(F32)).astype(BF16)

    def select(k):
        bytes_of(zbuf.at[k, pl.ds(0, NZ - 1)], z_recv.at[k])
        rows = jnp.concatenate([zbuf[k, z].astype(F32) for z in range(NZ)], axis=0).astype(BF16)
        picked = mm(smat[...], rows).astype(BF16)
        for x in range(NX):
            xsend[k, x] = picked[x * S:(x + 1) * S]
        for j in range(1, NX):
            x_copy(k, j).start()
        xbuf[k, my_x] = xsend[k, my_x]

    def gather_own(k):
        bytes_of(xbuf.at[k, pl.ds(0, NX - 1)], x_recv.at[k])
        rows = jnp.concatenate([xbuf[k, x] for x in range(NX)], axis=0)
        ybuf[k, blk_of(my_y)] = mm(pmat[...], rows).astype(BF16)
        y_copy(k, 0).start()
        y_copy(k, 1).start()
        s_copy(k, 0).start()

    def gather_near(k):
        bytes_of(ybuf.at[k, pl.ds(0, 2)], y_recv.at[k, 0])
        y_copy(k, 2).start()
        s_copy(k, 1).start()
        y_copy(k, 3).start()
        s_copy(k, 2).start()

    def gather_far(k):
        bytes_of(ybuf.at[k, 0], y_recv.at[k, 1])
        s_copy(k, 3).start()

    def multiply_up(k):
        bytes_of(ybuf.at[k, pl.ds(0, NY)], s_recv.at[k])
        w_rows = pl.ds(pl.multiple_of(k * C, 128), C)

        def rows_of(i, _):
            rows = ybuf[k, pl.ds(2 * i, 2)].reshape(2 * R, C)
            at = pl.ds(pl.multiple_of(i * 2 * R, 8), 2 * R)
            gacc[at] += mm(rows, wg[w_rows])
            uacc[at] += mm(rows, wu[w_rows])
            return 0

        lax.fori_loop(0, NC * NY // 2, rows_of, 0)

    request = (req * (NX * NZ) + ep) // 2
    heads = qbuf.shape[1]
    ctx = cachebuf.shape[2]

    def attend(i):
        q = qbuf[pl.ds(2 * i, 2)].reshape(2 * heads, qbuf.shape[2])
        near = jnp.concatenate([fresh[0].astype(F32), fresh[1].astype(F32)], axis=0).astype(BF16)
        held = []
        for h in range(2):
            part = mm(q, cachebuf[h]) * score_scale
            held.append(jnp.where(iota((2 * heads, ctx), 1) + h * ctx < clen[request], part, -jnp.inf))
        s_near = mm_nt(q, near) * score_scale
        seen = jnp.concatenate(
            [
                jnp.broadcast_to(vis[pl.ds(half * T + 2 * i + n, 1), :], (heads, 128))
                for n in range(2)
            ],
            axis=0,
        )[:, :2 * T]
        s_near = jnp.where(seen > 0.5, s_near, -jnp.inf)
        top = jnp.max(s_near, axis=1, keepdims=True)
        for part in held:
            top = jnp.maximum(top, jnp.max(part, axis=1, keepdims=True))
        p_near = jnp.exp(s_near - top)
        held = [jnp.exp(part - top) for part in held]
        total = jnp.sum(p_near, axis=1, keepdims=True)
        for part in held:
            total = total + jnp.sum(part, axis=1, keepdims=True)
        out = mm((p_near / total).astype(BF16), near[:, :VDIM])
        for h in range(2):
            out = out + mm_nt((held[h] / total).astype(BF16), cachebuf[h, 0:VDIM, :])
        obuf[pl.ds(2 * i, 2)] = out.astype(BF16).reshape(2, heads, VDIM)

    pieces = T // 2

    def dispatch_step(s, _):
        @pl.when(s + LEAD < K)
        def _():
            z_start(s + LEAD)

        @pl.when(s == CACHE_AT)
        def _():
            cache_copy.start()
            fresh_copy.start()

        @pl.when(s < K)
        def _():
            select(s)

        @pl.when(s == 0)
        def _():
            gacc[...] = jnp.zeros_like(gacc)
            uacc[...] = jnp.zeros_like(uacc)

        @pl.when((s >= 1) & (s < K + 1))
        def _():
            gather_own(s - 1)

        @pl.when((s >= NEAR) & (s < K + NEAR))
        def _():
            gather_near(s - NEAR)

        @pl.when(s == FAR)
        def _():
            local[0].wait()
            local[1].wait()

        @pl.when(s >= FAR)
        def _():
            gather_far(s - FAR)
            multiply_up(s - FAR)

        return 0

    lax.fori_loop(0, K + FAR, dispatch_step, 0)

    for i, core in enumerate((my_c, 1 - my_c)):
        for n, y in enumerate((far, nxt, prv, my_y)):
            at = pl.ds(pl.multiple_of((core * NY + y) * R, 8), R)
            gate = gacc[at]
            act[i, n] = (gate / (1.0 + jnp.exp(-gate)) * uacc[at]).astype(BF16)
    local[2].wait()

    def down_other(k):
        dsend[k, 0] = mm(act[1, 0], wd[:, cols(k)]).astype(BF16)
        d_copy(k, 0).start()
        rows = act[1, 1:NY].reshape((NY - 1) * R, FF)
        dsend[k, pl.ds(1, NY - 1)] = mm(rows, wd[:, cols(k)]).astype(BF16).reshape(NY - 1, R, C)
        d_copy(k, 1).start()

    def own_rows(k, n):
        return mm(act[0, n], wd[:, cols(k)]) + drecv[k, n].astype(F32)

    def send_far(k):
        d_copy(k, 0).wait_recv()
        rows = own_rows(k, 0).astype(BF16)
        r1send[k, 0] = rows[:HR]
        r1_copy(k, 0).start()
        r1send[k, 1] = rows[HR:]
        r1_copy(k, 1).start()

    def send_near(k):
        d_copy(k, 1).wait_recv()
        rows = own_rows(k, 1)
        bytes_of(r1recv.at[k], r1_recv.at[k])
        more = r1recv[k, 0].astype(F32)
        r2send[k, 0] = jnp.concatenate([rows[:HR] + more, rows[HR:]], axis=0).astype(BF16)
        r2_copy(k, 0).start()
        rows = own_rows(k, 2)
        more = r1recv[k, 1].astype(F32)
        r2send[k, 1] = jnp.concatenate([rows[:HR], rows[HR:] + more], axis=0).astype(BF16)
        r2_copy(k, 1).start()

    def send_back(k):
        rows = own_rows(k, 3)
        bytes_of(r2recv.at[k], r2_recv.at[k])
        rows = (rows + r2recv[k, 0].astype(F32) + r2recv[k, 1].astype(F32)).astype(BF16)
        spread = mm(emat[...], rows).astype(BF16)
        for x in range(NX):
            x2send[k, x] = spread[x * S:(x + 1) * S]
        for j in range(1, NX):
            x2_copy(k, j).start()
        x2buf[k, my_x] = x2send[k, my_x]

    def weigh(k):
        bytes_of(x2buf.at[k, pl.ds(0, NX - 1)], x2_recv.at[k])
        rows = jnp.concatenate([x2buf[k, x] for x in range(NX)], axis=0)
        sums = (mm(whi[...], rows) + mm(wlo[...], rows)).astype(BF16)
        for z in range(NZ):
            z2send[k, z] = sums[z * T:(z + 1) * T]
        for j in range(1, NZ):
            z2_copy(k, j).start()
        z2buf[k, my_z] = z2send[k, my_z]

    def finish(k):
        bytes_of(z2buf.at[k, pl.ds(0, NZ - 1)], z2_recv.at[k])
        rows = z2buf[k, 0].astype(F32)
        for z in range(1, NZ):
            rows = rows + z2buf[k, z].astype(F32)
        moe_out[:, cols(k)] = rows.astype(BF16)

    def tables():
        c_row, p_col = iota((XS, R), 0), iota((XS, R), 1)
        place = (c_row // S) * (NZ * CAP) + ((c_row % S) // PAD) * CAP + c_row % PAD
        emat[...] = jnp.where((place == p_col) & (c_row % PAD < CAP), 1.0, 0.0).astype(BF16)


        nodes = parents.shape[0]
        pick = iota(parents.shape, 1) == request
        par = jnp.sum(jnp.where(pick, parents[...], 0), axis=1, keepdims=True)
        par = jnp.concatenate([par, jnp.full((128 - nodes, 1), -1, jnp.int32)], axis=0)
        down, across = iota((128, 128), 0), iota((128, 128), 1)
        reach = jnp.where((down == across) | (across == par), 1.0, 0.0)
        for _ in range(4):
            reach = jnp.minimum(mm(reach.astype(BF16), reach.astype(BF16)), 1.0)
        vis[...] = reach[0:2 * T]

    def combine_step(s, _):
        @pl.when(s < K)
        def _():
            down_other(s)

        @pl.when((s >= COMB_FAR) & (s < K + COMB_FAR))
        def _():
            send_far(s - COMB_FAR)

        @pl.when(s == COMB_FAR)
        def _():
            tables()

        @pl.when((s >= COMB_NEAR) & (s < K + COMB_NEAR))
        def _():
            send_near(s - COMB_NEAR)

        @pl.when(s == ATTEND_AT)
        def _():
            local[3].wait()
            local[4].wait()
            cache_copy.wait_recv()
            fresh_copy.wait_recv()

        @pl.when((s >= COMB_BACK) & (s < K + COMB_BACK))
        def _():
            send_back(s - COMB_BACK)

        @pl.when((s >= ATTEND_AT) & (s < ATTEND_AT + pieces))
        def _():
            attend(s - ATTEND_AT)

        @pl.when(s == ATTEND_AT + pieces)
        def _():
            out_copy.start()

        @pl.when((s >= COMB_WEIGH) & (s < K + COMB_WEIGH))
        def _():
            weigh(s - COMB_WEIGH)

        @pl.when(s >= COMB_END)
        def _():
            finish(s - COMB_END)

        return 0

    out_copy = pltpu.make_async_copy(obuf, attn_out, out_sem)
    lax.fori_loop(0, K + COMB_END, combine_step, 0)
    bytes_of(metabuf.at[pl.ds(0, NZ - 1)], m_send)
    bytes_of(zbuf.at[:, pl.ds(0, NZ - 1)], z_send)
    bytes_of(xbuf.at[:, pl.ds(0, NX - 1)], x_send)
    bytes_of(ybuf.at[:, pl.ds(0, 3)], y_send)
    bytes_of(ybuf.at[:, pl.ds(0, NY)], s_send)
    bytes_of(drecv, d_send)
    bytes_of(r1recv, r1_send)
    bytes_of(r2recv, r2_send)
    bytes_of(x2buf.at[:, pl.ds(0, NX - 1)], x2_send)
    bytes_of(z2buf.at[:, pl.ds(0, NZ - 1)], z2_send)
    cache_copy.wait_send()
    fresh_copy.wait_send()
    out_copy.wait()


def body(queries, cache, newlat, parents, clen, tok, rid, rsc, wg, wu, wd):
    cache, parents = jnp.swapaxes(cache, 1, 2), parents.T
    T, D = tok.shape
    K = CHUNKS
    C = D // K
    S, R = NZ * PAD, NX * NZ * CAP
    HR = R // 2
    heads, lat = queries.shape[1:]
    FF = wg.shape[2]
    n_rows = NC * NY * R
    vmem, dma = pltpu.VMEM, pltpu.SemaphoreType.DMA
    anyspec, vspec = pl.BlockSpec(memory_space=pl.ANY), pl.BlockSpec(memory_space=pltpu.VMEM)
    scratch = [
        vmem((D, FF), BF16), vmem((D, FF), BF16), vmem((FF, D), BF16),
        vmem((T, heads, lat), BF16), vmem((2, lat, cache.shape[2]), BF16),
        vmem((2, T, lat), BF16), vmem((2 * T, 128), F32), vmem((T, heads, VDIM), BF16),
        vmem((2 * T, 128), F32), vmem((NZ, 2 * T, 128), F32),
        vmem((NX * S, NZ * T), BF16), vmem((R, NX * S), BF16), vmem((NX * S, R), BF16),
        vmem((NZ * T, NX * S), BF16), vmem((NZ * T, NX * S), BF16),
        vmem((K, NZ, T, C), BF16), vmem((K, NX, S, C), BF16), vmem((K, NX, S, C), BF16),
        vmem((K, NC * NY, R, C), BF16), vmem((n_rows, FF), F32), vmem((n_rows, FF), F32),
        vmem((NC, NY, R, FF), BF16),
        vmem((K, NY, R, C), BF16), vmem((K, NY, R, C), BF16),
        vmem((K, 2, HR, C), BF16), vmem((K, 2, HR, C), BF16),
        vmem((K, 2, R, C), BF16), vmem((K, 2, R, C), BF16),
        vmem((K, NX, S, C), BF16), vmem((K, NX, S, C), BF16),
        vmem((K, NZ, T, C), BF16), vmem((K, NZ, T, C), BF16),
        dma((5,)), dma, dma((2,)), dma((2,)), dma, dma,
        dma, dma((K,)), dma, dma((K,)), dma, dma((K, 2)), dma, dma((K,)),
        dma, dma((K, 2)), dma, dma((K,)), dma, dma((K,)), dma, dma((K,)), dma, dma((K,)),
    ]
    flops = 2 * n_rows * D * FF * 3 + 2 * T * heads * 2 * cache.shape[2] * (lat + VDIM)
    return tuple(pl.pallas_call(
        kernel,
        out_shape=(
            jax.ShapeDtypeStruct((T, heads, VDIM), BF16),
            jax.ShapeDtypeStruct((T, D), BF16),
        ),
        in_specs=[
            vspec, vspec, vspec, anyspec, anyspec, vspec, vspec,
            pl.BlockSpec(memory_space=pltpu.SMEM), anyspec, anyspec, anyspec,
        ],
        out_specs=(anyspec, vspec),
        scratch_shapes=scratch,
        compiler_params=pltpu.CompilerParams(
            collective_id=0, has_side_effects=True, vmem_limit_bytes=63 * 1024 * 1024
        ),
        cost_estimate=pl.CostEstimate(flops=flops, bytes_accessed=14_000_000, transcendentals=0),
        name="verify_layer",
    )(tok, rid, rsc, queries, cache, newlat, parents, clen, wg, wu, wd))


def solution(mesh):
    placed = (
        P(("req", "ep"), None, None),
        P(("req", "ep"), None, None),
        P(("req", "ep"), None),
        P(),
        P(),
        P(("req", "ep"), None),
        P(("req", "ep"), None),
        P(("req", "ep"), None),
        P("ep", None, "req"),
        P("ep", None, "req"),
        P("ep", "req", None),
    )
    return jax.shard_map(
        body,
        mesh=mesh,
        in_specs=placed,
        out_specs=(P(("req", "ep"), None, None), P(("req", "ep"), None)),
        check_vma=False,
    )
```

```python
import functools

import jax
import jax.numpy as jnp
from jax import lax
from jax.experimental import pallas as pl
from jax.experimental.pallas import tpu as pltpu
from jax.sharding import PartitionSpec as P

VDIM = 512
NX, NZ, NY, NC = 4, 8, 4, 2
CAP = 3
PAD = 4
CHUNKS = 7
Z_ORDER = sorted(range(1, NZ), key=lambda j: -min(j, NZ - j))
X_ORDER = sorted(range(1, NX), key=lambda j: -min(j, NX - j))
LEAD, NEAR, FAR = 2, 2, 3
COMB_FAR, COMB_NEAR, COMB_BACK, COMB_WEIGH, COMB_END = 0, 1, 2, 3, 4
CACHE_AT, ATTEND_AT = 5, 2

score_scale = 192.0 ** (-0.5)
route_scale = 2.5
F32, BF16 = jnp.float32, jnp.bfloat16
MESH = pl.DeviceIdType.MESH


def iota(shape, dim):
    return lax.broadcasted_iota(jnp.int32, shape, dim)


def mm(a, b):
    return jnp.dot(a, b, preferred_element_type=F32)


def mm_nt(a, b):
    return lax.dot_general(a, b, (((1,), (1,)), ((), ())), preferred_element_type=F32)


def kernel(
    tok, rid, rsc, queries, cache, newlat, parents, clen, wg_h, wu_h, wd_h,
    attn_out, moe_out,
    wg, wu, wd, qbuf, cachebuf, fresh, vis, obuf,
    msend, metabuf, smat, pmat, emat, whi, wlo,
    zbuf, xsend, xbuf, ybuf, gacc, uacc, act,
    dsend, drecv, r1send, r1recv, r2send, r2recv, x2send, x2buf, z2send, z2buf,
    loc_sem, out_sem, c_send, c_recv, m_send, m_recv,
    z_send, z_recv, x_send, x_recv, y_send, y_recv, s_send, s_recv,
    d_send, d_recv, r1_send, r1_recv, r2_send, r2_recv, x2_send, x2_recv, z2_send, z2_recv,
):
    req, ep = lax.axis_index("req"), lax.axis_index("ep")
    my_y, my_c = req // NC, req % NC
    my_x, my_z = ep // NZ, ep % NZ
    K = CHUNKS
    T = tok.shape[0]
    C = tok.shape[1] // K
    S = NZ * PAD
    R = NX * NZ * CAP
    HR = R // 2
    FF = wg.shape[1]
    rot = lambda a, j, n: lax.rem(a + j + n, n)
    nxt, prv, far = rot(my_y, 1, NY), rot(my_y, -1, NY), rot(my_y, 2, NY)
    dev_y = lambda y: (y * NC + my_c, ep)
    dev_x = lambda x: (req, x * NZ + my_z)
    dev_z = lambda z: (req, my_x * NZ + z)
    sib = (my_y * NC + (1 - my_c), ep)
    blk_of = lambda y: my_c * NY + y
    half = ep % 2
    mate = (req, ep + 1 - 2 * half)
    cols = lambda k: pl.ds(pl.multiple_of(k * C, 128), C)

    def remote(src, dst, ssem, rsem, device):
        return pltpu.make_async_remote_copy(
            src_ref=src, dst_ref=dst, send_sem=ssem, recv_sem=rsem,
            device_id=device, device_id_type=MESH,
        )

    def meta_copy(j):
        return remote(msend, metabuf.at[my_z], m_send, m_recv,
                      dev_z(rot(my_z, j, NZ)))

    def z_copy(k, j):
        return remote(tok.at[:, cols(k)], zbuf.at[k, my_z], z_send,
                      z_recv.at[k], dev_z(rot(my_z, j, NZ)))

    def x_copy(k, j):
        to = rot(my_x, j, NX)
        return remote(xsend.at[k, to], xbuf.at[k, my_x], x_send,
                      x_recv.at[k], dev_x(to))

    def y_copy(k, i):
        if i < 2:
            ref = ybuf.at[k, blk_of(my_y)]
        elif i == 2:
            ref = ybuf.at[k, blk_of(prv), pl.ds(0, HR)]
        else:
            ref = ybuf.at[k, blk_of(nxt), pl.ds(HR, HR)]
        return remote(ref, ref, y_send, y_recv.at[k, i // 2],
                      dev_y(nxt if i % 2 == 0 else prv))

    def s_copy(k, i):
        ref = ybuf.at[k, blk_of((my_y, prv, nxt, far)[i])]
        return remote(ref, ref, s_send, s_recv.at[k], sib)

    def d_copy(k, i):
        part = pl.ds(0, 1) if i == 0 else pl.ds(1, NY - 1)
        return remote(dsend.at[k, part], drecv.at[k, part], d_send, d_recv.at[k, i], sib)

    def r1_copy(k, i):
        return remote(r1send.at[k, i], r1recv.at[k, i], r1_send, r1_recv.at[k],
                      dev_y(nxt if i == 0 else prv))

    def r2_copy(k, i):
        return remote(r2send.at[k, i], r2recv.at[k, i], r2_send, r2_recv.at[k],
                      dev_y(nxt if i == 0 else prv))

    def x2_copy(k, j):
        to = rot(my_x, j, NX)
        return remote(x2send.at[k, to], x2buf.at[k, my_x], x2_send,
                      x2_recv.at[k], dev_x(to))

    def z2_copy(k, j):
        to = rot(my_z, j, NZ)
        return remote(z2send.at[k, to], z2buf.at[k, my_z], z2_send,
                      z2_recv.at[k], dev_z(to))

    def bytes_of(ref, sem):
        pltpu.make_async_copy(ref, ref, sem).wait()

    cache_copy = remote(cache.at[0], cachebuf.at[half], c_send.at[0], c_recv.at[0], mate)
    fresh_copy = remote(newlat, fresh.at[half], c_send.at[1], c_recv.at[1], mate)
    local = [
        pltpu.make_async_copy(wg_h.at[0], wg, loc_sem.at[0]),
        pltpu.make_async_copy(wu_h.at[0], wu, loc_sem.at[1]),
        pltpu.make_async_copy(wd_h.at[0], wd, loc_sem.at[2]),
        pltpu.make_async_copy(queries, qbuf, loc_sem.at[3]),
        pltpu.make_async_copy(cache.at[0], cachebuf.at[half], loc_sem.at[4]),
    ]

    barrier = pltpu.get_barrier_semaphore()
    peers = [dev_z(rot(my_z, j, NZ)) for j in range(1, NZ)]
    peers += [dev_x(rot(my_x, j, NX)) for j in range(1, NX)]
    peers += [dev_y(nxt), dev_y(prv), sib]
    for peer in peers:
        pl.semaphore_signal(barrier, inc=1, device_id=peer, device_id_type=MESH)
    msend[...] = jnp.zeros_like(msend)
    msend[0:T, 0:rid.shape[1]] = rid[...].astype(F32)
    scores = rsc[...]
    msend[T:2 * T, 0:rid.shape[1]] = route_scale * scores / jnp.sum(scores, axis=1, keepdims=True)
    metabuf[my_z] = msend[...]
    for copy in local:
        copy.start()
    fresh[half] = newlat[...]
    XS = NX * S
    c_row, p_col = iota((R, XS), 1), iota((R, XS), 0)
    place = (c_row // S) * (NZ * CAP) + ((c_row % S) // PAD) * CAP + c_row % PAD
    pmat[...] = jnp.where((place == p_col) & (c_row % PAD < CAP), 1.0, 0.0).astype(BF16)
    pl.semaphore_wait(barrier, len(peers))

    def z_start(k):
        for j in Z_ORDER:
            z_copy(k, j).start()
        zbuf[k, my_z] = tok[:, cols(k)]

    for j in Z_ORDER:
        meta_copy(j).start()
    for k in range(LEAD):
        z_start(k)

    bytes_of(metabuf.at[pl.ds(0, NZ - 1)], m_recv)
    L = NZ * T
    ids = jnp.concatenate([metabuf[z, 0:T] for z in range(NZ)], axis=0)
    wts = jnp.concatenate([metabuf[z, T:2 * T] for z in range(NZ)], axis=0)
    slot, line = iota((L, XS), 1), iota((L, XS), 0)
    expert = ((slot // S) * NZ + my_z).astype(F32)
    named, weight = jnp.zeros((L, XS), F32), jnp.zeros((L, XS), F32)
    for top in range(rid.shape[1]):
        hit = ids[:, top:top + 1] == expert
        named = jnp.where(hit, 1.0, named)
        weight = jnp.where(hit, wts[:, top:top + 1], weight)
    r0, r1 = iota((L, L), 0), iota((L, L), 1)
    before = jnp.where((r0 // T == r1 // T) & (r1 < r0), 1.0, 0.0).astype(BF16)
    rank = mm(before, named.astype(BF16))
    mine = (named > 0.5) & ((slot % S) // PAD == line // T) & (rank == (slot % PAD).astype(F32))
    smat[...] = jnp.transpose(jnp.where(mine, 1.0, 0.0)).astype(BF16)
    weight = jnp.where(mine, weight, 0.0)
    high = weight.astype(BF16)
    whi[...] = high
    wlo[...] = (weight - high.astype(F32)).astype(BF16)

    def select(k):
        bytes_of(zbuf.at[k, pl.ds(0, NZ - 1)], z_recv.at[k])
        rows = jnp.concatenate([zbuf[k, z].astype(F32) for z in range(NZ)], axis=0).astype(BF16)
        picked = mm(smat[...], rows).astype(BF16)
        for x in range(NX):
            xsend[k, x] = picked[x * S:(x + 1) * S]
        for j in X_ORDER:
            x_copy(k, j).start()
        xbuf[k, my_x] = xsend[k, my_x]

    def gather_own(k):
        bytes_of(xbuf.at[k, pl.ds(0, NX - 1)], x_recv.at[k])
        rows = jnp.concatenate([xbuf[k, x] for x in range(NX)], axis=0)
        ybuf[k, blk_of(my_y)] = mm(pmat[...], rows).astype(BF16)
        y_copy(k, 0).start()
        y_copy(k, 1).start()
        s_copy(k, 0).start()

    def gather_near(k):
        bytes_of(ybuf.at[k, pl.ds(0, 2)], y_recv.at[k, 0])
        y_copy(k, 2).start()
        s_copy(k, 1).start()
        y_copy(k, 3).start()
        s_copy(k, 2).start()

    def gather_far(k):
        bytes_of(ybuf.at[k, 0], y_recv.at[k, 1])
        s_copy(k, 3).start()

    def multiply_up(k):
        w_rows = pl.ds(pl.multiple_of(k * C, 128), C)

        def rows_of(i, _):
            rows = ybuf[k, pl.ds(2 * i, 2)].reshape(2 * R, C)
            at = pl.ds(pl.multiple_of(i * 2 * R, 8), 2 * R)
            gacc[at] += mm(rows, wg[w_rows])
            uacc[at] += mm(rows, wu[w_rows])
            return 0

        pairs = NY // 2
        lax.fori_loop(my_c * pairs, my_c * pairs + pairs, rows_of, 0)
        bytes_of(ybuf.at[k, pl.ds(0, NY)], s_recv.at[k])
        lax.fori_loop((1 - my_c) * pairs, (1 - my_c) * pairs + pairs, rows_of, 0)

    request = (req * (NX * NZ) + ep) // 2
    heads = qbuf.shape[1]
    ctx = cachebuf.shape[2]

    def attend(i):
        q = qbuf[pl.ds(2 * i, 2)].reshape(2 * heads, qbuf.shape[2])
        near = jnp.concatenate([fresh[0].astype(F32), fresh[1].astype(F32)], axis=0).astype(BF16)
        held = []
        for h in range(2):
            part = mm(q, cachebuf[h]) * score_scale
            held.append(jnp.where(iota((2 * heads, ctx), 1) + h * ctx < clen[request], part, -jnp.inf))
        s_near = mm_nt(q, near) * score_scale
        seen = jnp.concatenate(
            [
                jnp.broadcast_to(vis[pl.ds(half * T + 2 * i + n, 1), :], (heads, 128))
                for n in range(2)
            ],
            axis=0,
        )[:, :2 * T]
        s_near = jnp.where(seen > 0.5, s_near, -jnp.inf)
        top = jnp.max(s_near, axis=1, keepdims=True)
        for part in held:
            top = jnp.maximum(top, jnp.max(part, axis=1, keepdims=True))
        p_near = jnp.exp(s_near - top)
        held = [jnp.exp(part - top) for part in held]
        total = jnp.sum(p_near, axis=1, keepdims=True)
        for part in held:
            total = total + jnp.sum(part, axis=1, keepdims=True)
        out = mm((p_near / total).astype(BF16), near[:, :VDIM])
        for h in range(2):
            out = out + mm_nt((held[h] / total).astype(BF16), cachebuf[h, 0:VDIM, :])
        obuf[pl.ds(2 * i, 2)] = out.astype(BF16).reshape(2, heads, VDIM)

    pieces = T // 2

    def dispatch_step(s, _):
        @pl.when(s + LEAD < K)
        def _():
            z_start(s + LEAD)

        @pl.when(s == CACHE_AT)
        def _():
            cache_copy.start()
            fresh_copy.start()

        @pl.when((s >= 1) & (s < K + 1))
        def _():
            gather_own(s - 1)

        @pl.when(s < K)
        def _():
            select(s)

        @pl.when(s == 0)
        def _():
            gacc[...] = jnp.zeros_like(gacc)
            uacc[...] = jnp.zeros_like(uacc)

        @pl.when((s >= NEAR) & (s < K + NEAR))
        def _():
            gather_near(s - NEAR)

        @pl.when(s == FAR)
        def _():
            local[0].wait()
            local[1].wait()

        @pl.when(s >= FAR)
        def _():
            gather_far(s - FAR)
            multiply_up(s - FAR)

        return 0

    lax.fori_loop(0, K + FAR, dispatch_step, 0)

    def activate(i, core):
        for n, y in enumerate((far, nxt, prv, my_y)):
            at = pl.ds(pl.multiple_of((core * NY + y) * R, 8), R)
            gate = gacc[at]
            act[i, n] = (gate / (1.0 + jnp.exp(-gate)) * uacc[at]).astype(BF16)

    def down_other(k):
        dsend[k, 0] = mm(act[1, 0], wd[:, cols(k)]).astype(BF16)
        d_copy(k, 0).start()
        rows = act[1, 1:NY].reshape((NY - 1) * R, FF)
        dsend[k, pl.ds(1, NY - 1)] = mm(rows, wd[:, cols(k)]).astype(BF16).reshape(NY - 1, R, C)
        d_copy(k, 1).start()

    def own_rows(k, n):
        return mm(act[0, n], wd[:, cols(k)]) + drecv[k, n].astype(F32)

    def send_far(k):
        d_copy(k, 0).wait_recv()
        rows = own_rows(k, 0).astype(BF16)
        r1send[k, 0] = rows[:HR]
        r1_copy(k, 0).start()
        r1send[k, 1] = rows[HR:]
        r1_copy(k, 1).start()

    def send_near(k):
        d_copy(k, 1).wait_recv()
        rows = own_rows(k, 1)
        bytes_of(r1recv.at[k], r1_recv.at[k])
        more = r1recv[k, 0].astype(F32)
        r2send[k, 0] = jnp.concatenate([rows[:HR] + more, rows[HR:]], axis=0).astype(BF16)
        r2_copy(k, 0).start()
        rows = own_rows(k, 2)
        more = r1recv[k, 1].astype(F32)
        r2send[k, 1] = jnp.concatenate([rows[:HR], rows[HR:] + more], axis=0).astype(BF16)
        r2_copy(k, 1).start()

    def send_back(k):
        rows = own_rows(k, 3)
        bytes_of(r2recv.at[k], r2_recv.at[k])
        rows = (rows + r2recv[k, 0].astype(F32) + r2recv[k, 1].astype(F32)).astype(BF16)
        spread = mm(emat[...], rows).astype(BF16)
        for x in range(NX):
            x2send[k, x] = spread[x * S:(x + 1) * S]
        for j in X_ORDER:
            x2_copy(k, j).start()
        x2buf[k, my_x] = x2send[k, my_x]

    def weigh(k):
        bytes_of(x2buf.at[k, pl.ds(0, NX - 1)], x2_recv.at[k])
        rows = jnp.concatenate([x2buf[k, x] for x in range(NX)], axis=0)
        sums = (mm(whi[...], rows) + mm(wlo[...], rows)).astype(BF16)
        for z in range(NZ):
            z2send[k, z] = sums[z * T:(z + 1) * T]
        for j in Z_ORDER:
            z2_copy(k, j).start()
        z2buf[k, my_z] = z2send[k, my_z]

    def finish(k):
        bytes_of(z2buf.at[k, pl.ds(0, NZ - 1)], z2_recv.at[k])
        rows = z2buf[k, 0].astype(F32)
        for z in range(1, NZ):
            rows = rows + z2buf[k, z].astype(F32)
        moe_out[:, cols(k)] = rows.astype(BF16)

    def tables():
        c_row, p_col = iota((XS, R), 0), iota((XS, R), 1)
        place = (c_row // S) * (NZ * CAP) + ((c_row % S) // PAD) * CAP + c_row % PAD
        emat[...] = jnp.where((place == p_col) & (c_row % PAD < CAP), 1.0, 0.0).astype(BF16)


        nodes = parents.shape[0]
        pick = iota(parents.shape, 1) == request
        par = jnp.sum(jnp.where(pick, parents[...], 0), axis=1, keepdims=True)
        par = jnp.concatenate([par, jnp.full((128 - nodes, 1), -1, jnp.int32)], axis=0)
        down, across = iota((128, 128), 0), iota((128, 128), 1)
        reach = jnp.where((down == across) | (across == par), 1.0, 0.0)
        for _ in range(4):
            reach = jnp.minimum(mm(reach.astype(BF16), reach.astype(BF16)), 1.0)
        vis[...] = reach[0:2 * T]

    def combine_step(s, _):
        @pl.when((s >= COMB_FAR) & (s < K + COMB_FAR))
        def _():
            send_far(s - COMB_FAR)

        @pl.when(s + 1 < K)
        def _():
            down_other(s + 1)

        @pl.when((s >= COMB_NEAR) & (s < K + COMB_NEAR))
        def _():
            send_near(s - COMB_NEAR)

        @pl.when(s == COMB_NEAR)
        def _():
            tables()

        @pl.when(s == ATTEND_AT)
        def _():
            local[3].wait()
            local[4].wait()
            cache_copy.wait_recv()
            fresh_copy.wait_recv()

        @pl.when((s >= COMB_BACK) & (s < K + COMB_BACK))
        def _():
            send_back(s - COMB_BACK)

        @pl.when((s >= ATTEND_AT) & (s < ATTEND_AT + pieces))
        def _():
            attend(s - ATTEND_AT)

        @pl.when(s == ATTEND_AT + pieces)
        def _():
            out_copy.start()

        @pl.when((s >= COMB_WEIGH) & (s < K + COMB_WEIGH))
        def _():
            weigh(s - COMB_WEIGH)

        @pl.when(s >= COMB_END)
        def _():
            finish(s - COMB_END)

        return 0

    out_copy = pltpu.make_async_copy(obuf, attn_out, out_sem)
    activate(1, 1 - my_c)
    local[2].wait()
    down_other(0)
    activate(0, my_c)
    lax.fori_loop(0, K + COMB_END, combine_step, 0)
    bytes_of(metabuf.at[pl.ds(0, NZ - 1)], m_send)
    bytes_of(zbuf.at[:, pl.ds(0, NZ - 1)], z_send)
    bytes_of(xbuf.at[:, pl.ds(0, NX - 1)], x_send)
    bytes_of(ybuf.at[:, pl.ds(0, 3)], y_send)
    bytes_of(ybuf.at[:, pl.ds(0, NY)], s_send)
    bytes_of(drecv, d_send)
    bytes_of(r1recv, r1_send)
    bytes_of(r2recv, r2_send)
    bytes_of(x2buf.at[:, pl.ds(0, NX - 1)], x2_send)
    bytes_of(z2buf.at[:, pl.ds(0, NZ - 1)], z2_send)
    cache_copy.wait_send()
    fresh_copy.wait_send()
    out_copy.wait()


def keep(attended, summed, attn_out, moe_out):
    attn_out[...] = attended[...]
    moe_out[...] = summed[...]


def body(queries, cache, newlat, parents, clen, tok, rid, rsc, wg, wu, wd):
    cache, parents = jnp.swapaxes(cache, 1, 2), parents.T
    T, D = tok.shape
    K = CHUNKS
    C = D // K
    S, R = NZ * PAD, NX * NZ * CAP
    HR = R // 2
    heads, lat = queries.shape[1:]
    FF = wg.shape[2]
    n_rows = NC * NY * R
    vmem, dma = pltpu.VMEM, pltpu.SemaphoreType.DMA
    anyspec, vspec = pl.BlockSpec(memory_space=pl.ANY), pl.BlockSpec(memory_space=pltpu.VMEM)
    scratch = [
        vmem((D, FF), BF16), vmem((D, FF), BF16), vmem((FF, D), BF16),
        vmem((T, heads, lat), BF16), vmem((2, lat, cache.shape[2]), BF16),
        vmem((2, T, lat), BF16), vmem((2 * T, 128), F32), vmem((T, heads, VDIM), BF16),
        vmem((2 * T, 128), F32), vmem((NZ, 2 * T, 128), F32),
        vmem((NX * S, NZ * T), BF16), vmem((R, NX * S), BF16), vmem((NX * S, R), BF16),
        vmem((NZ * T, NX * S), BF16), vmem((NZ * T, NX * S), BF16),
        vmem((K, NZ, T, C), BF16), vmem((K, NX, S, C), BF16), vmem((K, NX, S, C), BF16),
        vmem((K, NC * NY, R, C), BF16), vmem((n_rows, FF), F32), vmem((n_rows, FF), F32),
        vmem((NC, NY, R, FF), BF16),
        vmem((K, NY, R, C), BF16), vmem((K, NY, R, C), BF16),
        vmem((K, 2, HR, C), BF16), vmem((K, 2, HR, C), BF16),
        vmem((K, 2, R, C), BF16), vmem((K, 2, R, C), BF16),
        vmem((K, NX, S, C), BF16), vmem((K, NX, S, C), BF16),
        vmem((K, NZ, T, C), BF16), vmem((K, NZ, T, C), BF16),
        dma((5,)), dma, dma((2,)), dma((2,)), dma, dma,
        dma, dma((K,)), dma, dma((K,)), dma, dma((K, 2)), dma, dma((K,)),
        dma, dma((K, 2)), dma, dma((K,)), dma, dma((K,)), dma, dma((K,)), dma, dma((K,)),
    ]
    flops = 2 * n_rows * D * FF * 3 + 2 * T * heads * 2 * cache.shape[2] * (lat + VDIM)
    attended, summed = pl.pallas_call(
        kernel,
        out_shape=(
            jax.ShapeDtypeStruct((T, heads, VDIM), BF16),
            jax.ShapeDtypeStruct((T, D), BF16),
        ),
        in_specs=[
            vspec, vspec, vspec, anyspec, anyspec, vspec, vspec,
            pl.BlockSpec(memory_space=pltpu.SMEM), anyspec, anyspec, anyspec,
        ],
        out_specs=(anyspec, vspec),
        scratch_shapes=scratch,
        compiler_params=pltpu.CompilerParams(
            collective_id=0, has_side_effects=True, vmem_limit_bytes=63 * 1024 * 1024
        ),
        cost_estimate=pl.CostEstimate(flops=flops, bytes_accessed=14_000_000, transcendentals=0),
        name="verify_layer",
    )(tok, rid, rsc, queries, cache, newlat, parents, clen, wg, wu, wd)
    return tuple(pl.pallas_call(
        keep,
        out_shape=(
            jax.ShapeDtypeStruct(attended.shape, BF16), jax.ShapeDtypeStruct(summed.shape, BF16)
        ),
        in_specs=[vspec, vspec],
        out_specs=(vspec, vspec),
        name="keep_results",
    )(attended, summed))


def solution(mesh):
    placed = (
        P(("req", "ep"), None, None),
        P(("req", "ep"), None, None),
        P(("req", "ep"), None),
        P(),
        P(),
        P(("req", "ep"), None),
        P(("req", "ep"), None),
        P(("req", "ep"), None),
        P("ep", None, "req"),
        P("ep", None, "req"),
        P("ep", "req", None),
    )
    return jax.shard_map(
        body,
        mesh=mesh,
        in_specs=placed,
        out_specs=(P(("req", "ep"), None, None), P(("req", "ep"), None)),
        check_vma=False,
    )
```

```python
import functools

import jax
import jax.numpy as jnp
from jax import lax
from jax.experimental import pallas as pl
from jax.experimental.pallas import tpu as pltpu
from jax.sharding import PartitionSpec as P

VDIM = 512
NX, NZ, NY, NC = 4, 8, 4, 2
CAP = 3
PAD = 4
CHUNKS = 7
Z_ORDER = sorted(range(1, NZ), key=lambda j: -min(j, NZ - j))
X_ORDER = sorted(range(1, NX), key=lambda j: -min(j, NX - j))
LEAD, NEAR, FAR = 2, 2, 4
COMB_FAR, COMB_NEAR, COMB_BACK, COMB_WEIGH, COMB_END = 0, 1, 2, 3, 4
CACHE_AT, ATTEND_AT = 5, 2

score_scale = 192.0 ** (-0.5)
route_scale = 2.5
F32, BF16 = jnp.float32, jnp.bfloat16
MESH = pl.DeviceIdType.MESH


def iota(shape, dim):
    return lax.broadcasted_iota(jnp.int32, shape, dim)


def mm(a, b):
    return jnp.dot(a, b, preferred_element_type=F32)


def mm_nt(a, b):
    return lax.dot_general(a, b, (((1,), (1,)), ((), ())), preferred_element_type=F32)


def kernel(
    tok, rid, rsc, queries, cache, newlat, parents, clen, wg_h, wu_h, wd_h,
    attn_out, moe_out,
    wg, wu, wd, qbuf, cachebuf, fresh, vis, obuf,
    msend, metabuf, smat, pmat, emat, whi, wlo,
    zbuf, xsend, xbuf, ybuf, gacc, uacc, act,
    dsend, drecv, r1send, r1recv, r2send, r2recv, x2send, x2buf, z2send, z2buf,
    loc_sem, out_sem, c_send, c_recv, m_send, m_recv,
    z_send, z_recv, x_send, x_recv, y_send, y_recv, s_send, s_recv,
    d_send, d_recv, r1_send, r1_recv, r2_send, r2_recv, x2_send, x2_recv, z2_send, z2_recv,
):
    req, ep = lax.axis_index("req"), lax.axis_index("ep")
    my_y, my_c = req // NC, req % NC
    my_x, my_z = ep // NZ, ep % NZ
    K = CHUNKS
    T = tok.shape[0]
    C = tok.shape[1] // K
    S = NZ * PAD
    R = NX * NZ * CAP
    HR = R // 2
    FF = wg.shape[1]
    rot = lambda a, j, n: lax.rem(a + j + n, n)
    nxt, prv, far = rot(my_y, 1, NY), rot(my_y, -1, NY), rot(my_y, 2, NY)
    dev_y = lambda y: (y * NC + my_c, ep)
    dev_x = lambda x: (req, x * NZ + my_z)
    dev_z = lambda z: (req, my_x * NZ + z)
    sib = (my_y * NC + (1 - my_c), ep)
    blk_of = lambda y: my_c * NY + y
    half = ep % 2
    mate = (req, ep + 1 - 2 * half)
    cols = lambda k: pl.ds(pl.multiple_of(k * C, 128), C)

    def remote(src, dst, ssem, rsem, device):
        return pltpu.make_async_remote_copy(
            src_ref=src, dst_ref=dst, send_sem=ssem, recv_sem=rsem,
            device_id=device, device_id_type=MESH,
        )

    def meta_copy(j):
        return remote(msend, metabuf.at[my_z], m_send, m_recv,
                      dev_z(rot(my_z, j, NZ)))

    def z_copy(k, j):
        return remote(tok.at[:, cols(k)], zbuf.at[k, my_z], z_send,
                      z_recv.at[k], dev_z(rot(my_z, j, NZ)))

    def x_copy(k, j):
        to = rot(my_x, j, NX)
        return remote(xsend.at[k, to], xbuf.at[k, my_x], x_send,
                      x_recv.at[k], dev_x(to))

    def y_copy(k, i):
        y = my_y if i < 4 else (prv, nxt)[i - 4]
        ref = ybuf.at[k, blk_of(y), pl.ds((0, HR, HR, 0, 0, HR)[i], HR)]
        return remote(ref, ref, y_send, y_recv.at[k, i // 2],
                      dev_y(nxt if i % 2 == 0 else prv))

    def s_copy(k, i):
        ref = ybuf.at[k, blk_of((my_y, prv, nxt, far)[i])]
        return remote(ref, ref, s_send, s_recv.at[k], sib)

    def d_copy(k, i):
        part = pl.ds(0, 1) if i == 0 else pl.ds(1, NY - 1)
        return remote(dsend.at[k, part], drecv.at[k, part], d_send, d_recv.at[k, i], sib)

    def r1_copy(k, i):
        return remote(r1send.at[k, i], r1recv.at[k, i], r1_send, r1_recv.at[k],
                      dev_y(nxt if i == 0 else prv))

    def r2_copy(k, i):
        return remote(r2send.at[k, i], r2recv.at[k, i], r2_send, r2_recv.at[k],
                      dev_y(nxt if i == 0 else prv))

    def x2_copy(k, j):
        to = rot(my_x, j, NX)
        return remote(x2send.at[k, to], x2buf.at[k, my_x], x2_send,
                      x2_recv.at[k], dev_x(to))

    def z2_copy(k, j):
        to = rot(my_z, j, NZ)
        return remote(z2send.at[k, to], z2buf.at[k, my_z], z2_send,
                      z2_recv.at[k], dev_z(to))

    def bytes_of(ref, sem):
        pltpu.make_async_copy(ref, ref, sem).wait()

    cache_copy = remote(cache.at[0], cachebuf.at[half], c_send.at[0], c_recv.at[0], mate)
    fresh_copy = remote(newlat, fresh.at[half], c_send.at[1], c_recv.at[1], mate)
    local = [
        pltpu.make_async_copy(wg_h.at[0], wg, loc_sem.at[0]),
        pltpu.make_async_copy(wu_h.at[0], wu, loc_sem.at[1]),
        pltpu.make_async_copy(wd_h.at[0], wd, loc_sem.at[2]),
        pltpu.make_async_copy(queries, qbuf, loc_sem.at[3]),
        pltpu.make_async_copy(cache.at[0], cachebuf.at[half], loc_sem.at[4]),
    ]

    barrier = pltpu.get_barrier_semaphore()
    peers = [dev_z(rot(my_z, j, NZ)) for j in range(1, NZ)]
    peers += [dev_x(rot(my_x, j, NX)) for j in range(1, NX)]
    peers += [dev_y(nxt), dev_y(prv), sib]
    for peer in peers:
        pl.semaphore_signal(barrier, inc=1, device_id=peer, device_id_type=MESH)
    msend[...] = jnp.zeros_like(msend)
    msend[0:T, 0:rid.shape[1]] = rid[...].astype(F32)
    scores = rsc[...]
    msend[T:2 * T, 0:rid.shape[1]] = route_scale * scores / jnp.sum(scores, axis=1, keepdims=True)
    metabuf[my_z] = msend[...]
    for copy in local:
        copy.start()
    fresh[half] = newlat[...]
    XS = NX * S
    c_row, p_col = iota((R, XS), 1), iota((R, XS), 0)
    place = (c_row // S) * (NZ * CAP) + ((c_row % S) // PAD) * CAP + c_row % PAD
    pmat[...] = jnp.where((place == p_col) & (c_row % PAD < CAP), 1.0, 0.0).astype(BF16)
    pl.semaphore_wait(barrier, len(peers))

    def z_start(k):
        for j in Z_ORDER:
            z_copy(k, j).start()
        zbuf[k, my_z] = tok[:, cols(k)]

    for j in Z_ORDER:
        meta_copy(j).start()
    for k in range(LEAD):
        z_start(k)

    bytes_of(metabuf.at[pl.ds(0, NZ - 1)], m_recv)
    L = NZ * T
    ids = jnp.concatenate([metabuf[z, 0:T] for z in range(NZ)], axis=0)
    wts = jnp.concatenate([metabuf[z, T:2 * T] for z in range(NZ)], axis=0)
    slot, line = iota((L, XS), 1), iota((L, XS), 0)
    expert = ((slot // S) * NZ + my_z).astype(F32)
    named, weight = jnp.zeros((L, XS), F32), jnp.zeros((L, XS), F32)
    for top in range(rid.shape[1]):
        hit = ids[:, top:top + 1] == expert
        named = jnp.where(hit, 1.0, named)
        weight = jnp.where(hit, wts[:, top:top + 1], weight)
    r0, r1 = iota((L, L), 0), iota((L, L), 1)
    before = jnp.where((r0 // T == r1 // T) & (r1 < r0), 1.0, 0.0).astype(BF16)
    rank = mm(before, named.astype(BF16))
    mine = (named > 0.5) & ((slot % S) // PAD == line // T) & (rank == (slot % PAD).astype(F32))
    smat[...] = jnp.transpose(jnp.where(mine, 1.0, 0.0)).astype(BF16)
    weight = jnp.where(mine, weight, 0.0)
    high = weight.astype(BF16)
    whi[...] = high
    wlo[...] = (weight - high.astype(F32)).astype(BF16)

    def select(k):
        bytes_of(zbuf.at[k, pl.ds(0, NZ - 1)], z_recv.at[k])
        rows = jnp.concatenate([zbuf[k, z].astype(F32) for z in range(NZ)], axis=0).astype(BF16)
        picked = mm(smat[...], rows).astype(BF16)
        for x in range(NX):
            xsend[k, x] = picked[x * S:(x + 1) * S]
        for j in X_ORDER:
            x_copy(k, j).start()
        xbuf[k, my_x] = xsend[k, my_x]

    def gather_own(k):
        bytes_of(xbuf.at[k, pl.ds(0, NX - 1)], x_recv.at[k])
        rows = jnp.concatenate([xbuf[k, x] for x in range(NX)], axis=0)
        ybuf[k, blk_of(my_y)] = mm(pmat[...], rows).astype(BF16)
        for i in range(4):
            y_copy(k, i).start()
        s_copy(k, 0).start()

    def gather_near(k):
        bytes_of(ybuf.at[k, 0], y_recv.at[k, 0])
        y_copy(k, 4).start()
        y_copy(k, 5).start()
        bytes_of(ybuf.at[k, 0], y_recv.at[k, 1])
        s_copy(k, 1).start()
        s_copy(k, 2).start()

    def gather_far(k):
        bytes_of(ybuf.at[k, 0], y_recv.at[k, 2])
        s_copy(k, 3).start()

    def multiply_up(k):
        w_rows = pl.ds(pl.multiple_of(k * C, 128), C)

        def rows_of(i, _):
            rows = ybuf[k, pl.ds(2 * i, 2)].reshape(2 * R, C)
            at = pl.ds(pl.multiple_of(i * 2 * R, 8), 2 * R)
            gacc[at] += mm(rows, wg[w_rows])
            uacc[at] += mm(rows, wu[w_rows])
            return 0

        pairs = NY // 2
        lax.fori_loop(my_c * pairs, my_c * pairs + pairs, rows_of, 0)
        bytes_of(ybuf.at[k, pl.ds(0, NY)], s_recv.at[k])
        lax.fori_loop((1 - my_c) * pairs, (1 - my_c) * pairs + pairs, rows_of, 0)

    request = (req * (NX * NZ) + ep) // 2
    heads = qbuf.shape[1]
    ctx = cachebuf.shape[2]

    def attend(i):
        q = qbuf[pl.ds(2 * i, 2)].reshape(2 * heads, qbuf.shape[2])
        near = jnp.concatenate([fresh[0].astype(F32), fresh[1].astype(F32)], axis=0).astype(BF16)
        held = []
        for h in range(2):
            part = mm(q, cachebuf[h]) * score_scale
            held.append(jnp.where(iota((2 * heads, ctx), 1) + h * ctx < clen[request], part, -jnp.inf))
        s_near = mm_nt(q, near) * score_scale
        seen = jnp.concatenate(
            [
                jnp.broadcast_to(vis[pl.ds(half * T + 2 * i + n, 1), :], (heads, 128))
                for n in range(2)
            ],
            axis=0,
        )[:, :2 * T]
        s_near = jnp.where(seen > 0.5, s_near, -jnp.inf)
        top = jnp.max(s_near, axis=1, keepdims=True)
        for part in held:
            top = jnp.maximum(top, jnp.max(part, axis=1, keepdims=True))
        p_near = jnp.exp(s_near - top)
        held = [jnp.exp(part - top) for part in held]
        total = jnp.sum(p_near, axis=1, keepdims=True)
        for part in held:
            total = total + jnp.sum(part, axis=1, keepdims=True)
        out = mm((p_near / total).astype(BF16), near[:, :VDIM])
        for h in range(2):
            out = out + mm_nt((held[h] / total).astype(BF16), cachebuf[h, 0:VDIM, :])
        obuf[pl.ds(2 * i, 2)] = out.astype(BF16).reshape(2, heads, VDIM)

    pieces = T // 2

    def dispatch_step(s, _):
        @pl.when(s + LEAD < K)
        def _():
            z_start(s + LEAD)

        @pl.when(s == CACHE_AT)
        def _():
            cache_copy.start()
            fresh_copy.start()

        @pl.when((s >= 1) & (s < K + 1))
        def _():
            gather_own(s - 1)

        @pl.when(s < K)
        def _():
            select(s)

        @pl.when(s == 0)
        def _():
            gacc[...] = jnp.zeros_like(gacc)
            uacc[...] = jnp.zeros_like(uacc)

        @pl.when((s >= NEAR) & (s < K + NEAR))
        def _():
            gather_near(s - NEAR)

        @pl.when(s == FAR)
        def _():
            local[0].wait()
            local[1].wait()

        @pl.when(s >= FAR)
        def _():
            gather_far(s - FAR)
            multiply_up(s - FAR)

        return 0

    lax.fori_loop(0, K + FAR, dispatch_step, 0)

    def activate(i, core):
        for n, y in enumerate((far, nxt, prv, my_y)):
            at = pl.ds(pl.multiple_of((core * NY + y) * R, 8), R)
            gate = gacc[at]
            act[i, n] = (gate / (1.0 + jnp.exp(-gate)) * uacc[at]).astype(BF16)

    def down_other(k):
        dsend[k, 0] = mm(act[1, 0], wd[:, cols(k)]).astype(BF16)
        d_copy(k, 0).start()
        rows = act[1, 1:NY].reshape((NY - 1) * R, FF)
        dsend[k, pl.ds(1, NY - 1)] = mm(rows, wd[:, cols(k)]).astype(BF16).reshape(NY - 1, R, C)
        d_copy(k, 1).start()

    def own_rows(k, n):
        return mm(act[0, n], wd[:, cols(k)]) + drecv[k, n].astype(F32)

    def send_far(k):
        d_copy(k, 0).wait_recv()
        rows = own_rows(k, 0).astype(BF16)
        r1send[k, 0] = rows[:HR]
        r1_copy(k, 0).start()
        r1send[k, 1] = rows[HR:]
        r1_copy(k, 1).start()

    def send_near(k):
        d_copy(k, 1).wait_recv()
        rows = own_rows(k, 1)
        bytes_of(r1recv.at[k], r1_recv.at[k])
        more = r1recv[k, 0].astype(F32)
        r2send[k, 0] = jnp.concatenate([rows[:HR] + more, rows[HR:]], axis=0).astype(BF16)
        r2_copy(k, 0).start()
        rows = own_rows(k, 2)
        more = r1recv[k, 1].astype(F32)
        r2send[k, 1] = jnp.concatenate([rows[:HR], rows[HR:] + more], axis=0).astype(BF16)
        r2_copy(k, 1).start()

    def send_back(k):
        rows = own_rows(k, 3)
        bytes_of(r2recv.at[k], r2_recv.at[k])
        rows = (rows + r2recv[k, 0].astype(F32) + r2recv[k, 1].astype(F32)).astype(BF16)
        spread = mm(emat[...], rows).astype(BF16)
        for x in range(NX):
            x2send[k, x] = spread[x * S:(x + 1) * S]
        for j in X_ORDER:
            x2_copy(k, j).start()
        x2buf[k, my_x] = x2send[k, my_x]

    def weigh(k):
        bytes_of(x2buf.at[k, pl.ds(0, NX - 1)], x2_recv.at[k])
        rows = jnp.concatenate([x2buf[k, x] for x in range(NX)], axis=0)
        sums = (mm(whi[...], rows) + mm(wlo[...], rows)).astype(BF16)
        for z in range(NZ):
            z2send[k, z] = sums[z * T:(z + 1) * T]
        for j in Z_ORDER:
            z2_copy(k, j).start()
        z2buf[k, my_z] = z2send[k, my_z]

    def finish(k):
        bytes_of(z2buf.at[k, pl.ds(0, NZ - 1)], z2_recv.at[k])
        rows = z2buf[k, 0].astype(F32)
        for z in range(1, NZ):
            rows = rows + z2buf[k, z].astype(F32)
        moe_out[:, cols(k)] = rows.astype(BF16)

    def tables():
        c_row, p_col = iota((XS, R), 0), iota((XS, R), 1)
        place = (c_row // S) * (NZ * CAP) + ((c_row % S) // PAD) * CAP + c_row % PAD
        emat[...] = jnp.where((place == p_col) & (c_row % PAD < CAP), 1.0, 0.0).astype(BF16)


        nodes = parents.shape[0]
        pick = iota(parents.shape, 1) == request
        par = jnp.sum(jnp.where(pick, parents[...], 0), axis=1, keepdims=True)
        par = jnp.concatenate([par, jnp.full((128 - nodes, 1), -1, jnp.int32)], axis=0)
        down, across = iota((128, 128), 0), iota((128, 128), 1)
        reach = jnp.where((down == across) | (across == par), 1.0, 0.0)
        for _ in range(4):
            reach = jnp.minimum(mm(reach.astype(BF16), reach.astype(BF16)), 1.0)
        vis[...] = reach[0:2 * T]

    def combine_step(s, _):
        @pl.when((s >= COMB_FAR) & (s < K + COMB_FAR))
        def _():
            send_far(s - COMB_FAR)

        @pl.when(s + 1 < K)
        def _():
            down_other(s + 1)

        @pl.when((s >= COMB_NEAR) & (s < K + COMB_NEAR))
        def _():
            send_near(s - COMB_NEAR)

        @pl.when(s == COMB_NEAR)
        def _():
            tables()

        @pl.when(s == ATTEND_AT)
        def _():
            local[3].wait()
            local[4].wait()
            cache_copy.wait_recv()
            fresh_copy.wait_recv()

        @pl.when((s >= COMB_BACK) & (s < K + COMB_BACK))
        def _():
            send_back(s - COMB_BACK)

        @pl.when((s >= ATTEND_AT) & (s < ATTEND_AT + pieces))
        def _():
            attend(s - ATTEND_AT)

        @pl.when(s == ATTEND_AT + pieces)
        def _():
            out_copy.start()

        @pl.when((s >= COMB_WEIGH) & (s < K + COMB_WEIGH))
        def _():
            weigh(s - COMB_WEIGH)

        @pl.when(s >= COMB_END)
        def _():
            finish(s - COMB_END)

        return 0

    out_copy = pltpu.make_async_copy(obuf, attn_out, out_sem)
    activate(1, 1 - my_c)
    local[2].wait()
    down_other(0)
    activate(0, my_c)
    lax.fori_loop(0, K + COMB_END, combine_step, 0)
    bytes_of(metabuf.at[pl.ds(0, NZ - 1)], m_send)
    bytes_of(zbuf.at[:, pl.ds(0, NZ - 1)], z_send)
    bytes_of(xbuf.at[:, pl.ds(0, NX - 1)], x_send)
    bytes_of(ybuf.at[:, pl.ds(0, 3)], y_send)
    bytes_of(ybuf.at[:, pl.ds(0, NY)], s_send)
    bytes_of(drecv, d_send)
    bytes_of(r1recv, r1_send)
    bytes_of(r2recv, r2_send)
    bytes_of(x2buf.at[:, pl.ds(0, NX - 1)], x2_send)
    bytes_of(z2buf.at[:, pl.ds(0, NZ - 1)], z2_send)
    cache_copy.wait_send()
    fresh_copy.wait_send()
    out_copy.wait()


def keep(attended, summed, attn_out, moe_out):
    attn_out[...] = attended[...]
    moe_out[...] = summed[...]


def body(queries, cache, newlat, parents, clen, tok, rid, rsc, wg, wu, wd):
    cache, parents = jnp.swapaxes(cache, 1, 2), parents.T
    T, D = tok.shape
    K = CHUNKS
    C = D // K
    S, R = NZ * PAD, NX * NZ * CAP
    HR = R // 2
    heads, lat = queries.shape[1:]
    FF = wg.shape[2]
    n_rows = NC * NY * R
    vmem, dma = pltpu.VMEM, pltpu.SemaphoreType.DMA
    anyspec, vspec = pl.BlockSpec(memory_space=pl.ANY), pl.BlockSpec(memory_space=pltpu.VMEM)
    scratch = [
        vmem((D, FF), BF16), vmem((D, FF), BF16), vmem((FF, D), BF16),
        vmem((T, heads, lat), BF16), vmem((2, lat, cache.shape[2]), BF16),
        vmem((2, T, lat), BF16), vmem((2 * T, 128), F32), vmem((T, heads, VDIM), BF16),
        vmem((2 * T, 128), F32), vmem((NZ, 2 * T, 128), F32),
        vmem((NX * S, NZ * T), BF16), vmem((R, NX * S), BF16), vmem((NX * S, R), BF16),
        vmem((NZ * T, NX * S), BF16), vmem((NZ * T, NX * S), BF16),
        vmem((K, NZ, T, C), BF16), vmem((K, NX, S, C), BF16), vmem((K, NX, S, C), BF16),
        vmem((K, NC * NY, R, C), BF16), vmem((n_rows, FF), F32), vmem((n_rows, FF), F32),
        vmem((NC, NY, R, FF), BF16),
        vmem((K, NY, R, C), BF16), vmem((K, NY, R, C), BF16),
        vmem((K, 2, HR, C), BF16), vmem((K, 2, HR, C), BF16),
        vmem((K, 2, R, C), BF16), vmem((K, 2, R, C), BF16),
        vmem((K, NX, S, C), BF16), vmem((K, NX, S, C), BF16),
        vmem((K, NZ, T, C), BF16), vmem((K, NZ, T, C), BF16),
        dma((5,)), dma, dma((2,)), dma((2,)), dma, dma,
        dma, dma((K,)), dma, dma((K,)), dma, dma((K, 3)), dma, dma((K,)),
        dma, dma((K, 2)), dma, dma((K,)), dma, dma((K,)), dma, dma((K,)), dma, dma((K,)),
    ]
    flops = 2 * n_rows * D * FF * 3 + 2 * T * heads * 2 * cache.shape[2] * (lat + VDIM)
    attended, summed = pl.pallas_call(
        kernel,
        out_shape=(
            jax.ShapeDtypeStruct((T, heads, VDIM), BF16),
            jax.ShapeDtypeStruct((T, D), BF16),
        ),
        in_specs=[
            vspec, vspec, vspec, anyspec, anyspec, vspec, vspec,
            pl.BlockSpec(memory_space=pltpu.SMEM), anyspec, anyspec, anyspec,
        ],
        out_specs=(anyspec, vspec),
        scratch_shapes=scratch,
        compiler_params=pltpu.CompilerParams(
            collective_id=0, has_side_effects=True, vmem_limit_bytes=63 * 1024 * 1024
        ),
        cost_estimate=pl.CostEstimate(flops=flops, bytes_accessed=14_000_000, transcendentals=0),
        name="verify_layer",
    )(tok, rid, rsc, queries, cache, newlat, parents, clen, wg, wu, wd)
    return tuple(pl.pallas_call(
        keep,
        out_shape=(
            jax.ShapeDtypeStruct(attended.shape, BF16), jax.ShapeDtypeStruct(summed.shape, BF16)
        ),
        in_specs=[vspec, vspec],
        out_specs=(vspec, vspec),
        name="keep_results",
    )(attended, summed))


def solution(mesh):
    placed = (
        P(("req", "ep"), None, None),
        P(("req", "ep"), None, None),
        P(("req", "ep"), None),
        P(),
        P(),
        P(("req", "ep"), None),
        P(("req", "ep"), None),
        P(("req", "ep"), None),
        P("ep", None, "req"),
        P("ep", None, "req"),
        P("ep", "req", None),
    )
    return jax.shard_map(
        body,
        mesh=mesh,
        in_specs=placed,
        out_specs=(P(("req", "ep"), None, None), P(("req", "ep"), None)),
        check_vma=False,
    )
```

```python
import functools

import jax
import jax.numpy as jnp
from jax import lax
from jax.experimental import pallas as pl
from jax.experimental.pallas import tpu as pltpu
from jax.sharding import PartitionSpec as P

VDIM = 512
NX, NZ, NY, NC = 4, 8, 4, 2
CAP = 3
PAD = 4
CHUNKS = 7
Z_ORDER = sorted(range(1, NZ), key=lambda j: -min(j, NZ - j))
X_ORDER = sorted(range(1, NX), key=lambda j: -min(j, NX - j))
LEAD, NEAR, FAR = 2, 2, 4
COMB_FAR, COMB_NEAR, COMB_BACK, COMB_WEIGH, COMB_END = 0, 1, 2, 3, 4
CACHE_AT, ATTEND_AT = 5, 2

score_scale = 192.0 ** (-0.5)
route_scale = 2.5
F32, BF16 = jnp.float32, jnp.bfloat16
MESH = pl.DeviceIdType.MESH


def iota(shape, dim):
    return lax.broadcasted_iota(jnp.int32, shape, dim)


def mm(a, b):
    return jnp.dot(a, b, preferred_element_type=F32)


def mm_nt(a, b):
    return lax.dot_general(a, b, (((1,), (1,)), ((), ())), preferred_element_type=F32)


def kernel(
    tok, rid, rsc, queries, cache, newlat, parents, clen, wg_h, wu_h, wd_h,
    attn_out, moe_out,
    wg, wu, wd, qbuf, cachebuf, fresh, vis, obuf,
    msend, metabuf, smat, pmat, emat, whi, wlo,
    zbuf, xsend, xbuf, ybuf, gacc, uacc, act,
    dsend, drecv, r1send, r1recv, r2send, r2recv, x2send, x2buf, z2send, z2buf,
    loc_sem, out_sem, c_send, c_recv, m_send, m_recv,
    z_send, z_recv, x_send, x_recv, y_send, y_recv, s_send, s_recv,
    d_send, d_recv, r1_send, r1_recv, r2_send, r2_recv, x2_send, x2_recv, z2_send, z2_recv,
):
    req, ep = lax.axis_index("req"), lax.axis_index("ep")
    my_y, my_c = req // NC, req % NC
    my_x, my_z = ep // NZ, ep % NZ
    K = CHUNKS
    T = tok.shape[0]
    C = tok.shape[1] // K
    S = NZ * PAD
    R = NX * NZ * CAP
    HR = R // 2
    FF = wg.shape[1]
    rot = lambda a, j, n: lax.rem(a + j + n, n)
    nxt, prv, far = rot(my_y, 1, NY), rot(my_y, -1, NY), rot(my_y, 2, NY)
    dev_y = lambda y: (y * NC + my_c, ep)
    dev_x = lambda x: (req, x * NZ + my_z)
    dev_z = lambda z: (req, my_x * NZ + z)
    sib = (my_y * NC + (1 - my_c), ep)
    blk_of = lambda y: my_c * NY + y
    half = ep % 2
    mate = (req, ep + 1 - 2 * half)
    cols = lambda k: pl.ds(pl.multiple_of(k * C, 128), C)

    def remote(src, dst, ssem, rsem, device):
        return pltpu.make_async_remote_copy(
            src_ref=src, dst_ref=dst, send_sem=ssem, recv_sem=rsem,
            device_id=device, device_id_type=MESH,
        )

    def meta_copy(j):
        return remote(msend, metabuf.at[my_z], m_send, m_recv,
                      dev_z(rot(my_z, j, NZ)))

    def z_copy(k, j):
        return remote(tok.at[:, cols(k)], zbuf.at[k, my_z], z_send,
                      z_recv.at[k], dev_z(rot(my_z, j, NZ)))

    def x_copy(k, j):
        to = rot(my_x, j, NX)
        return remote(xsend.at[k, to], xbuf.at[k, my_x], x_send,
                      x_recv.at[k], dev_x(to))

    def y_copy(k, i):
        y = my_y if i < 4 else (prv, nxt)[i - 4]
        ref = ybuf.at[k, blk_of(y), pl.ds((0, HR, HR, 0, 0, HR)[i], HR)]
        return remote(ref, ref, y_send, y_recv.at[k, i // 2],
                      dev_y(nxt if i % 2 == 0 else prv))

    def s_copy(k, i):
        ref = ybuf.at[k, blk_of((my_y, prv, nxt, far)[i])]
        return remote(ref, ref, s_send, s_recv.at[k], sib)

    def d_copy(k, i):
        part = pl.ds(0, 1) if i == 0 else pl.ds(1, NY - 1)
        return remote(dsend.at[k, part], drecv.at[k, part], d_send, d_recv.at[k, i], sib)

    def r1_copy(k, i):
        return remote(r1send.at[k, i], r1recv.at[k, i], r1_send, r1_recv.at[k],
                      dev_y(nxt if i == 0 else prv))

    def r2_copy(k, i, h):
        part = pl.ds(h * HR, HR)
        return remote(r2send.at[k, i, part], r2recv.at[k, i, part], r2_send, r2_recv.at[k],
                      dev_y(nxt if i == 0 else prv))

    def x2_copy(k, j):
        to = rot(my_x, j, NX)
        return remote(x2send.at[k, to], x2buf.at[k, my_x], x2_send,
                      x2_recv.at[k], dev_x(to))

    def z2_copy(k, j):
        to = rot(my_z, j, NZ)
        return remote(z2send.at[k, to], z2buf.at[k, my_z], z2_send,
                      z2_recv.at[k], dev_z(to))

    def bytes_of(ref, sem):
        pltpu.make_async_copy(ref, ref, sem).wait()

    cache_copy = remote(cache.at[0], cachebuf.at[half], c_send.at[0], c_recv.at[0], mate)
    fresh_copy = remote(newlat, fresh.at[half], c_send.at[1], c_recv.at[1], mate)
    local = [
        pltpu.make_async_copy(wg_h.at[0], wg, loc_sem.at[0]),
        pltpu.make_async_copy(wu_h.at[0], wu, loc_sem.at[1]),
        pltpu.make_async_copy(wd_h.at[0], wd, loc_sem.at[2]),
        pltpu.make_async_copy(queries, qbuf, loc_sem.at[3]),
        pltpu.make_async_copy(cache.at[0], cachebuf.at[half], loc_sem.at[4]),
    ]

    barrier = pltpu.get_barrier_semaphore()
    peers = [dev_z(rot(my_z, j, NZ)) for j in range(1, NZ)]
    peers += [dev_x(rot(my_x, j, NX)) for j in range(1, NX)]
    peers += [dev_y(nxt), dev_y(prv), sib]
    for peer in peers:
        pl.semaphore_signal(barrier, inc=1, device_id=peer, device_id_type=MESH)
    msend[...] = jnp.zeros_like(msend)
    msend[0:T, 0:rid.shape[1]] = rid[...].astype(F32)
    scores = rsc[...]
    msend[T:2 * T, 0:rid.shape[1]] = route_scale * scores / jnp.sum(scores, axis=1, keepdims=True)
    metabuf[my_z] = msend[...]
    for copy in local:
        copy.start()
    fresh[half] = newlat[...]
    XS = NX * S
    c_row, p_col = iota((R, XS), 1), iota((R, XS), 0)
    place = (c_row // S) * (NZ * CAP) + ((c_row % S) // PAD) * CAP + c_row % PAD
    pmat[...] = jnp.where((place == p_col) & (c_row % PAD < CAP), 1.0, 0.0).astype(BF16)
    pl.semaphore_wait(barrier, len(peers))

    def z_start(k):
        for j in Z_ORDER:
            z_copy(k, j).start()
        zbuf[k, my_z] = tok[:, cols(k)]

    for j in Z_ORDER:
        meta_copy(j).start()
    for k in range(LEAD):
        z_start(k)

    bytes_of(metabuf.at[pl.ds(0, NZ - 1)], m_recv)
    L = NZ * T
    ids = jnp.concatenate([metabuf[z, 0:T] for z in range(NZ)], axis=0)
    wts = jnp.concatenate([metabuf[z, T:2 * T] for z in range(NZ)], axis=0)
    slot, line = iota((L, XS), 1), iota((L, XS), 0)
    expert = ((slot // S) * NZ + my_z).astype(F32)
    named, weight = jnp.zeros((L, XS), F32), jnp.zeros((L, XS), F32)
    for top in range(rid.shape[1]):
        hit = ids[:, top:top + 1] == expert
        named = jnp.where(hit, 1.0, named)
        weight = jnp.where(hit, wts[:, top:top + 1], weight)
    r0, r1 = iota((L, L), 0), iota((L, L), 1)
    before = jnp.where((r0 // T == r1 // T) & (r1 < r0), 1.0, 0.0).astype(BF16)
    rank = mm(before, named.astype(BF16))
    mine = (named > 0.5) & ((slot % S) // PAD == line // T) & (rank == (slot % PAD).astype(F32))
    smat[...] = jnp.transpose(jnp.where(mine, 1.0, 0.0)).astype(BF16)
    weight = jnp.where(mine, weight, 0.0)
    high = weight.astype(BF16)
    whi[...] = high
    wlo[...] = (weight - high.astype(F32)).astype(BF16)

    def select(k):
        bytes_of(zbuf.at[k, pl.ds(0, NZ - 1)], z_recv.at[k])
        rows = jnp.concatenate([zbuf[k, z].astype(F32) for z in range(NZ)], axis=0).astype(BF16)
        picked = mm(smat[...], rows).astype(BF16)
        for x in range(NX):
            xsend[k, x] = picked[x * S:(x + 1) * S]
        for j in X_ORDER:
            x_copy(k, j).start()
        xbuf[k, my_x] = xsend[k, my_x]

    def gather_own(k):
        bytes_of(xbuf.at[k, pl.ds(0, NX - 1)], x_recv.at[k])
        rows = jnp.concatenate([xbuf[k, x] for x in range(NX)], axis=0)
        ybuf[k, blk_of(my_y)] = mm(pmat[...], rows).astype(BF16)
        for i in range(4):
            y_copy(k, i).start()
        s_copy(k, 0).start()

    def gather_near(k):
        bytes_of(ybuf.at[k, 0], y_recv.at[k, 0])
        y_copy(k, 4).start()
        y_copy(k, 5).start()
        bytes_of(ybuf.at[k, 0], y_recv.at[k, 1])
        s_copy(k, 1).start()
        s_copy(k, 2).start()

    def gather_far(k):
        bytes_of(ybuf.at[k, 0], y_recv.at[k, 2])
        s_copy(k, 3).start()

    def multiply_up(k):
        w_rows = pl.ds(pl.multiple_of(k * C, 128), C)

        def rows_of(i, _):
            rows = ybuf[k, pl.ds(2 * i, 2)].reshape(2 * R, C)
            at = pl.ds(pl.multiple_of(i * 2 * R, 8), 2 * R)
            gacc[at] += mm(rows, wg[w_rows])
            uacc[at] += mm(rows, wu[w_rows])
            return 0

        pairs = NY // 2
        lax.fori_loop(my_c * pairs, my_c * pairs + pairs, rows_of, 0)
        bytes_of(ybuf.at[k, pl.ds(0, NY)], s_recv.at[k])
        lax.fori_loop((1 - my_c) * pairs, (1 - my_c) * pairs + pairs, rows_of, 0)

    request = (req * (NX * NZ) + ep) // 2
    heads = qbuf.shape[1]
    ctx = cachebuf.shape[2]

    def attend(i):
        q = qbuf[pl.ds(2 * i, 2)].reshape(2 * heads, qbuf.shape[2])
        near = jnp.concatenate([fresh[0].astype(F32), fresh[1].astype(F32)], axis=0).astype(BF16)
        held = []
        for h in range(2):
            part = mm(q, cachebuf[h]) * score_scale
            held.append(jnp.where(iota((2 * heads, ctx), 1) + h * ctx < clen[request], part, -jnp.inf))
        s_near = mm_nt(q, near) * score_scale
        seen = jnp.concatenate(
            [
                jnp.broadcast_to(vis[pl.ds(half * T + 2 * i + n, 1), :], (heads, 128))
                for n in range(2)
            ],
            axis=0,
        )[:, :2 * T]
        s_near = jnp.where(seen > 0.5, s_near, -jnp.inf)
        top = jnp.max(s_near, axis=1, keepdims=True)
        for part in held:
            top = jnp.maximum(top, jnp.max(part, axis=1, keepdims=True))
        p_near = jnp.exp(s_near - top)
        held = [jnp.exp(part - top) for part in held]
        total = jnp.sum(p_near, axis=1, keepdims=True)
        for part in held:
            total = total + jnp.sum(part, axis=1, keepdims=True)
        out = mm((p_near / total).astype(BF16), near[:, :VDIM])
        for h in range(2):
            out = out + mm_nt((held[h] / total).astype(BF16), cachebuf[h, 0:VDIM, :])
        obuf[pl.ds(2 * i, 2)] = out.astype(BF16).reshape(2, heads, VDIM)

    pieces = T // 2

    def dispatch_step(s, _):
        @pl.when(s + LEAD < K)
        def _():
            z_start(s + LEAD)

        @pl.when(s == CACHE_AT)
        def _():
            cache_copy.start()
            fresh_copy.start()

        @pl.when((s >= 1) & (s < K + 1))
        def _():
            gather_own(s - 1)

        @pl.when(s < K)
        def _():
            select(s)

        @pl.when(s == 0)
        def _():
            gacc[...] = jnp.zeros_like(gacc)
            uacc[...] = jnp.zeros_like(uacc)

        @pl.when((s >= NEAR) & (s < K + NEAR))
        def _():
            gather_near(s - NEAR)

        @pl.when(s == FAR)
        def _():
            local[0].wait()
            local[1].wait()

        @pl.when(s >= FAR)
        def _():
            gather_far(s - FAR)
            multiply_up(s - FAR)

        return 0

    lax.fori_loop(0, K + FAR, dispatch_step, 0)

    def activate(i, core):
        for n, y in enumerate((far, nxt, prv, my_y)):
            at = pl.ds(pl.multiple_of((core * NY + y) * R, 8), R)
            gate = gacc[at]
            act[i, n] = (gate / (1.0 + jnp.exp(-gate)) * uacc[at]).astype(BF16)

    def down_other(k):
        dsend[k, 0] = mm(act[1, 0], wd[:, cols(k)]).astype(BF16)
        d_copy(k, 0).start()
        rows = act[1, 1:NY].reshape((NY - 1) * R, FF)
        dsend[k, pl.ds(1, NY - 1)] = mm(rows, wd[:, cols(k)]).astype(BF16).reshape(NY - 1, R, C)
        d_copy(k, 1).start()

    def own_rows(k, n):
        return mm(act[0, n], wd[:, cols(k)]) + drecv[k, n].astype(F32)

    def send_far(k):
        d_copy(k, 0).wait_recv()
        rows = own_rows(k, 0).astype(BF16)
        r1send[k, 0] = rows[:HR]
        r1_copy(k, 0).start()
        r1send[k, 1] = rows[HR:]
        r1_copy(k, 1).start()

        bytes_of(drecv.at[k, pl.ds(1, NY - 1)], d_recv.at[k, 1])
        for i in range(2):
            r2send[k, i, pl.ds((1 - i) * HR, HR)] = half_rows(k, i + 1, 1 - i).astype(BF16)
            r2_copy(k, i, 1 - i).start()

    def half_rows(k, n, h):
        part = pl.ds(h * HR, HR)
        return mm(act[0, n, part], wd[:, cols(k)]) + drecv[k, n, part].astype(F32)

    def send_near(k):
        bytes_of(r1recv.at[k], r1_recv.at[k])
        for i in range(2):
            rows = half_rows(k, i + 1, i) + r1recv[k, i].astype(F32)
            r2send[k, i, pl.ds(i * HR, HR)] = rows.astype(BF16)
            r2_copy(k, i, i).start()

    def send_back(k):
        rows = own_rows(k, 3)
        bytes_of(r2recv.at[k], r2_recv.at[k])
        rows = (rows + r2recv[k, 0].astype(F32) + r2recv[k, 1].astype(F32)).astype(BF16)
        spread = mm(emat[...], rows).astype(BF16)
        for x in range(NX):
            x2send[k, x] = spread[x * S:(x + 1) * S]
        for j in X_ORDER:
            x2_copy(k, j).start()
        x2buf[k, my_x] = x2send[k, my_x]

    def weigh(k):
        bytes_of(x2buf.at[k, pl.ds(0, NX - 1)], x2_recv.at[k])
        rows = jnp.concatenate([x2buf[k, x] for x in range(NX)], axis=0)
        sums = (mm(whi[...], rows) + mm(wlo[...], rows)).astype(BF16)
        for z in range(NZ):
            z2send[k, z] = sums[z * T:(z + 1) * T]
        for j in Z_ORDER:
            z2_copy(k, j).start()
        z2buf[k, my_z] = z2send[k, my_z]

    def finish(k):
        bytes_of(z2buf.at[k, pl.ds(0, NZ - 1)], z2_recv.at[k])
        rows = z2buf[k, 0].astype(F32)
        for z in range(1, NZ):
            rows = rows + z2buf[k, z].astype(F32)
        moe_out[:, cols(k)] = rows.astype(BF16)

    def tables():
        c_row, p_col = iota((XS, R), 0), iota((XS, R), 1)
        place = (c_row // S) * (NZ * CAP) + ((c_row % S) // PAD) * CAP + c_row % PAD
        emat[...] = jnp.where((place == p_col) & (c_row % PAD < CAP), 1.0, 0.0).astype(BF16)


        nodes = parents.shape[0]
        pick = iota(parents.shape, 1) == request
        par = jnp.sum(jnp.where(pick, parents[...], 0), axis=1, keepdims=True)
        par = jnp.concatenate([par, jnp.full((128 - nodes, 1), -1, jnp.int32)], axis=0)
        down, across = iota((128, 128), 0), iota((128, 128), 1)
        reach = jnp.where((down == across) | (across == par), 1.0, 0.0)
        for _ in range(4):
            reach = jnp.minimum(mm(reach.astype(BF16), reach.astype(BF16)), 1.0)
        vis[...] = reach[0:2 * T]

    def combine_step(s, _):
        @pl.when((s >= COMB_FAR) & (s < K + COMB_FAR))
        def _():
            send_far(s - COMB_FAR)

        @pl.when(s + 1 < K)
        def _():
            down_other(s + 1)

        @pl.when((s >= COMB_NEAR) & (s < K + COMB_NEAR))
        def _():
            send_near(s - COMB_NEAR)

        @pl.when(s == COMB_NEAR)
        def _():
            tables()

        @pl.when(s == ATTEND_AT)
        def _():
            local[3].wait()
            local[4].wait()
            cache_copy.wait_recv()
            fresh_copy.wait_recv()

        @pl.when((s >= COMB_BACK) & (s < K + COMB_BACK))
        def _():
            send_back(s - COMB_BACK)

        @pl.when((s >= ATTEND_AT) & (s < ATTEND_AT + pieces))
        def _():
            attend(s - ATTEND_AT)

        @pl.when(s == ATTEND_AT + pieces)
        def _():
            out_copy.start()

        @pl.when((s >= COMB_WEIGH) & (s < K + COMB_WEIGH))
        def _():
            weigh(s - COMB_WEIGH)

        @pl.when(s >= COMB_END)
        def _():
            finish(s - COMB_END)

        return 0

    out_copy = pltpu.make_async_copy(obuf, attn_out, out_sem)
    activate(1, 1 - my_c)
    local[2].wait()
    down_other(0)
    activate(0, my_c)
    lax.fori_loop(0, K + COMB_END, combine_step, 0)
    bytes_of(metabuf.at[pl.ds(0, NZ - 1)], m_send)
    bytes_of(zbuf.at[:, pl.ds(0, NZ - 1)], z_send)
    bytes_of(xbuf.at[:, pl.ds(0, NX - 1)], x_send)
    bytes_of(ybuf.at[:, pl.ds(0, 3)], y_send)
    bytes_of(ybuf.at[:, pl.ds(0, NY)], s_send)
    bytes_of(drecv, d_send)
    bytes_of(r1recv, r1_send)
    bytes_of(r2recv, r2_send)
    bytes_of(x2buf.at[:, pl.ds(0, NX - 1)], x2_send)
    bytes_of(z2buf.at[:, pl.ds(0, NZ - 1)], z2_send)
    cache_copy.wait_send()
    fresh_copy.wait_send()
    out_copy.wait()


def keep(attended, summed, attn_out, moe_out):
    attn_out[...] = attended[...]
    moe_out[...] = summed[...]


def body(queries, cache, newlat, parents, clen, tok, rid, rsc, wg, wu, wd):
    cache, parents = jnp.swapaxes(cache, 1, 2), parents.T
    T, D = tok.shape
    K = CHUNKS
    C = D // K
    S, R = NZ * PAD, NX * NZ * CAP
    HR = R // 2
    heads, lat = queries.shape[1:]
    FF = wg.shape[2]
    n_rows = NC * NY * R
    vmem, dma = pltpu.VMEM, pltpu.SemaphoreType.DMA
    anyspec, vspec = pl.BlockSpec(memory_space=pl.ANY), pl.BlockSpec(memory_space=pltpu.VMEM)
    scratch = [
        vmem((D, FF), BF16), vmem((D, FF), BF16), vmem((FF, D), BF16),
        vmem((T, heads, lat), BF16), vmem((2, lat, cache.shape[2]), BF16),
        vmem((2, T, lat), BF16), vmem((2 * T, 128), F32), vmem((T, heads, VDIM), BF16),
        vmem((2 * T, 128), F32), vmem((NZ, 2 * T, 128), F32),
        vmem((NX * S, NZ * T), BF16), vmem((R, NX * S), BF16), vmem((NX * S, R), BF16),
        vmem((NZ * T, NX * S), BF16), vmem((NZ * T, NX * S), BF16),
        vmem((K, NZ, T, C), BF16), vmem((K, NX, S, C), BF16), vmem((K, NX, S, C), BF16),
        vmem((K, NC * NY, R, C), BF16), vmem((n_rows, FF), F32), vmem((n_rows, FF), F32),
        vmem((NC, NY, R, FF), BF16),
        vmem((K, NY, R, C), BF16), vmem((K, NY, R, C), BF16),
        vmem((K, 2, HR, C), BF16), vmem((K, 2, HR, C), BF16),
        vmem((K, 2, R, C), BF16), vmem((K, 2, R, C), BF16),
        vmem((K, NX, S, C), BF16), vmem((K, NX, S, C), BF16),
        vmem((K, NZ, T, C), BF16), vmem((K, NZ, T, C), BF16),
        dma((5,)), dma, dma((2,)), dma((2,)), dma, dma,
        dma, dma((K,)), dma, dma((K,)), dma, dma((K, 3)), dma, dma((K,)),
        dma, dma((K, 2)), dma, dma((K,)), dma, dma((K,)), dma, dma((K,)), dma, dma((K,)),
    ]
    flops = 2 * n_rows * D * FF * 3 + 2 * T * heads * 2 * cache.shape[2] * (lat + VDIM)
    attended, summed = pl.pallas_call(
        kernel,
        out_shape=(
            jax.ShapeDtypeStruct((T, heads, VDIM), BF16),
            jax.ShapeDtypeStruct((T, D), BF16),
        ),
        in_specs=[
            vspec, vspec, vspec, anyspec, anyspec, vspec, vspec,
            pl.BlockSpec(memory_space=pltpu.SMEM), anyspec, anyspec, anyspec,
        ],
        out_specs=(anyspec, vspec),
        scratch_shapes=scratch,
        compiler_params=pltpu.CompilerParams(
            collective_id=0, has_side_effects=True, vmem_limit_bytes=63 * 1024 * 1024
        ),
        cost_estimate=pl.CostEstimate(flops=flops, bytes_accessed=14_000_000, transcendentals=0),
        name="verify_layer",
    )(tok, rid, rsc, queries, cache, newlat, parents, clen, wg, wu, wd)
    return tuple(pl.pallas_call(
        keep,
        out_shape=(
            jax.ShapeDtypeStruct(attended.shape, BF16), jax.ShapeDtypeStruct(summed.shape, BF16)
        ),
        in_specs=[vspec, vspec],
        out_specs=(vspec, vspec),
        name="keep_results",
    )(attended, summed))


def solution(mesh):
    placed = (
        P(("req", "ep"), None, None),
        P(("req", "ep"), None, None),
        P(("req", "ep"), None),
        P(),
        P(),
        P(("req", "ep"), None),
        P(("req", "ep"), None),
        P(("req", "ep"), None),
        P("ep", None, "req"),
        P("ep", None, "req"),
        P("ep", "req", None),
    )
    return jax.shard_map(
        body,
        mesh=mesh,
        in_specs=placed,
        out_specs=(P(("req", "ep"), None, None), P(("req", "ep"), None)),
        check_vma=False,
    )
```
